32 devices in a mesh: ctx: 8 (over z, x), tp: 4 (over y, core).
Axes of the slice: x: 2, y: 2, z: 4, core: 2. Of those that a mesh axis runs over, the one named last changes fastest.
Arguments:
- query_head_matrix: bfloat16 [1024, 4096], P('ctx', 'tp'), may hold values from -6 to 6
- key_head_matrix: bfloat16 [1024, 1024], P('ctx', 'tp'), may hold values from -6 to 6
- value_head_matrix: bfloat16 [1024, 1024], P('ctx', 'tp'), may hold values from -6 to 6
- ssm_input: bfloat16 [1024, 8192], P('ctx', 'tp'), may hold values from -0.59765625 to 0.59765625
- log_decay: float32 [1024, 128], P('ctx', 'tp'), may hold values from -1 to 0
- state_write: bfloat16 [1024, 128], P('ctx'), may hold values from -1.796875 to 1.796875
- state_read: bfloat16 [1024, 128], P('ctx'), may hold values from -1.796875 to 1.796875
- document_ids: int32 [1024], P('ctx'), may hold values from 0 to 7, never falling along the last dimension, each value on 1 to 256 neighbouring positions
- attention_output_gradient: bfloat16 [1024, 4096], P('ctx', 'tp'), may hold values from -6 to 6
- cot_mixer: bfloat16 [1024, 8192], P('ctx', 'tp'), may hold values from -6 to 6
Outputs:
- attention_out: bfloat16 [1024, 4096], P('ctx', 'tp')
- mixer_out: bfloat16 [1024, 8192], P('ctx', 'tp')
- grad_key: bfloat16 [1024, 1024], P('ctx', 'tp')
- grad_value: bfloat16 [1024, 1024], P('ctx', 'tp')
- grad_input: bfloat16 [1024, 8192], P('ctx', 'tp')
The draws below stay inside these ranges and needn't reach their ends.
Inputs may be any that keep to these rules, and one draw needn't show every extreme that they name: `document_ids`: never falls along the sequence; each document holds 1 to 256 tokens.
All inputs are finite; a program needn't handle non-finite values.
Results may differ from the reference program's by a relative error of at most 0.0062.
Values may be sent and summed in bfloat16 or wider, within the bound.
No kernel may reach another device: no remote copies, remote signals or barrier semaphores. Data moves between devices by JAX's collectives and lax.ppermute only.
A program may use at most 320 MiB of HBM per device.

```python
import math
import jax
import jax.numpy as jnp
import numpy as np
from jax import lax

QUERY_HEADS = 32
KEY_VALUE_HEADS = 8
HEAD_CHANNELS = 128
MIXER_HEADS = 128
SP = 64
SN = 128
TOK_DEV = 128
SPAN = 2
PACKED_TOKENS = 1024
LONGEST_DOCUMENT = 256
DOCS = 8
N_CTX = 8


def draw_key_head_matrix(key, part):
    random_base_key = jax.random.fold_in(key, 7002)
    base_values = jnp.clip(jax.random.normal(random_base_key, (PACKED_TOKENS, KEY_VALUE_HEADS, HEAD_CHANNELS), jnp.float32), -5.5, 5.5)
    return base_values.reshape(PACKED_TOKENS, KEY_VALUE_HEADS * HEAD_CHANNELS).astype(jnp.bfloat16)


def draw_query_head_matrix(key, part):
    queries_per_group = QUERY_HEADS // KEY_VALUE_HEADS
    random_base_key = jax.random.fold_in(key, 7003)
    base_values = jnp.clip(jax.random.normal(random_base_key, (PACKED_TOKENS, KEY_VALUE_HEADS, queries_per_group, HEAD_CHANNELS), jnp.float32), -5.5, 5.5)
    return base_values.reshape(PACKED_TOKENS, QUERY_HEADS * HEAD_CHANNELS).astype(jnp.bfloat16)


def draw_log_decay(key, part):
    rate_key = jax.random.fold_in(key, 7010)
    step_key = jax.random.fold_in(key, 7011)
    spike_random_key = jax.random.fold_in(key, 7012)
    size_key = jax.random.fold_in(key, 7013)
    spread = jax.random.uniform(rate_key, (MIXER_HEADS,), jnp.float32)
    low_log = math.log(0.1 / LONGEST_DOCUMENT)
    rates = jnp.exp(low_log + spread * math.log(LONGEST_DOCUMENT / 3.0))
    step_len = jax.random.uniform(step_key, (PACKED_TOKENS, MIXER_HEADS), jnp.float32, 0.5, 1.5)
    match_flags = jax.random.uniform(spike_random_key, (PACKED_TOKENS, MIXER_HEADS), jnp.float32) < 3.0 / LONGEST_DOCUMENT
    jumps = jnp.where(match_flags, jax.random.uniform(size_key, (PACKED_TOKENS, MIXER_HEADS), jnp.float32, 0.22, 0.69), 0.0)
    return -(rates[None, :] * step_len + jumps)


def shard_levels(key, dims, shards, low, largest):
    def one(axis_at, parts):
        draws = jax.random.uniform(jax.random.fold_in(jax.random.fold_in(key, 6), axis_at), (parts,), jnp.float32, low / len(shards), largest / len(shards))
        return jnp.repeat(jnp.exp(draws), dims[axis_at] // parts).reshape((-1,) + (1,) * (len(dims) - axis_at - 1))

    factor_of = one(*shards[0])
    for cut in shards[1:]:
        factor_of = factor_of * one(*cut)
    return factor_of


def profile(count, total, most, slope):
    weights = [(1 << 20) // math.isqrt(standing ** slope) + 1 for standing in range(2, count + 1)]
    surplus, counts = total - most - (count - 1), [1] * (count - 1)
    while surplus > 0:
        free = [i for i in range(count - 1) if counts[i] < most]
        whole, left = sum([weights[i] for i in free]), surplus
        for i in free:
            addition = min(most - counts[i], max(1, left * weights[i] // whole), surplus)
            counts[i] = counts[i] + addition
            surplus = surplus - addition
    return np.array([most] + counts)


def ragged_sizes(stream_key, count, total, most, skew):
    if count == 2:
        one = jax.random.randint(stream_key, (), max(1, total - most), min(most, total - 1) + 1)
        return jnp.stack([one, total - one])
    lengths = jnp.asarray(profile(count, total, most, skew), jnp.int32)
    twos = (count - 1) // 2
    giver, receiver = lengths[1:1 + 2 * twos:2], lengths[2:2 + 2 * twos:2]
    room = jnp.minimum(giver - 1, most - receiver)
    passed = jax.random.randint(jax.random.fold_in(stream_key, 1), (twos,), 0, 1 << 20) % (room + 1)
    lengths = lengths.at[1:1 + 2 * twos:2].set(giver - passed).at[2:2 + 2 * twos:2].set(receiver + passed)
    return lengths[jax.random.permutation(jax.random.fold_in(stream_key, 2), count)]


def normal_values(key, extent, width, bound, cuts=(), held_as=jnp.bfloat16):
    result = jax.random.normal(key, extent, jnp.float32) * width
    if len(cuts) > 0:
        result = shard_levels(key, extent, cuts, -0.22, 0.18) * result
    return jnp.clip(result, min=-bound, max=bound).astype(held_as)


def setup_inputs(seed: int = 0) -> dict:
    streams_of = jax.random.split(jax.random.key(seed), 11)
    query_head_matrix = draw_query_head_matrix(jax.random.fold_in(streams_of[10], 71), 0)
    key_head_matrix = draw_key_head_matrix(jax.random.fold_in(streams_of[10], 71), 0)
    value_head_matrix = normal_values(streams_of[2], (PACKED_TOKENS, KEY_VALUE_HEADS * HEAD_CHANNELS), 1.0, 6.0, ((0, 8), (1, 4)))
    ssm_input = normal_values(streams_of[3], (PACKED_TOKENS, MIXER_HEADS * SP), 0.1, 0.59765625, ((0, 8), (1, 4)))
    log_decay = draw_log_decay(jax.random.fold_in(streams_of[10], 71), 0)
    state_write = normal_values(streams_of[5], (PACKED_TOKENS, SN), 0.3, 1.796875, ((0, 8),))
    state_read = normal_values(streams_of[6], (PACKED_TOKENS, SN), 0.3, 1.796875, ((0, 8),))
    document_ids = jnp.searchsorted(jnp.cumsum(ragged_sizes(streams_of[7], DOCS, PACKED_TOKENS, LONGEST_DOCUMENT, 2)), jnp.arange(PACKED_TOKENS), side="right").astype(jnp.int32)
    attention_output_gradient = normal_values(streams_of[8], (PACKED_TOKENS, QUERY_HEADS * HEAD_CHANNELS), 1.0, 6.0, ((0, 8), (1, 4)))
    cot_mixer = normal_values(streams_of[9], (PACKED_TOKENS, MIXER_HEADS * SP), 1.0, 6.0, ((0, 8), (1, 4)))
    return {"query_head_matrix": query_head_matrix, "key_head_matrix": key_head_matrix, "value_head_matrix": value_head_matrix, "ssm_input": ssm_input, "log_decay": log_decay, "state_write": state_write, "state_read": state_read, "document_ids": document_ids, "attention_output_gradient": attention_output_gradient, "cot_mixer": cot_mixer}


def mixer_block_pieces(decays, writes, reads, doc_row, prev_doc):
    tokens = decays.shape[0]
    running = jnp.cumsum(decays, axis=0).T
    row_ids = jnp.arange(tokens)
    inside = (row_ids[:, None] >= row_ids[None, :]) & (doc_row[:, None] == doc_row[None, :])
    log_gaps = running[:, :, None] - running[:, None, :]
    decay_mat = jnp.exp(jnp.where(inside[None], log_gaps, -jnp.inf))
    scores = jnp.dot(reads, writes.T, preferred_element_type=jnp.float32)
    weights = (decay_mat * scores[None]).astype(jnp.bfloat16)
    entry_w = jnp.exp(running) * (doc_row == prev_doc).astype(jnp.float32)[None]
    read_w = (entry_w[:, :, None] * reads.astype(jnp.float32)[None]).astype(jnp.bfloat16)
    exit_w = jnp.exp(running[:, -1:] - running) * (doc_row == doc_row[-1]).astype(jnp.float32)[None]
    write_w = (exit_w[:, :, None] * writes.astype(jnp.float32)[None]).astype(jnp.bfloat16)
    block_gain = jnp.exp(running[:, -1]) * (doc_row[-1] == prev_doc).astype(jnp.float32)
    weights, read_w, write_w = lax.optimization_barrier((weights, read_w, write_w))
    return (weights, read_w, write_w, block_gain)

def mixer_reference(ssm_input, log_decay, state_write, state_read, document_ids, cot_mixer):
    blocks = N_CTX
    input_blocks = ssm_input.reshape(blocks, TOK_DEV, MIXER_HEADS, SP)
    cot_blocks = cot_mixer.reshape(blocks, TOK_DEV, MIXER_HEADS, SP)
    decay_blocks = log_decay.reshape(blocks, TOK_DEV, MIXER_HEADS)
    write_blocks = state_write.reshape(blocks, TOK_DEV, SN)
    read_blocks = state_read.reshape(blocks, TOK_DEV, SN)
    doc_blocks = document_ids.reshape(blocks, TOK_DEV)
    prev_docs = jnp.concatenate([jnp.full((1,), -1, jnp.int32), doc_blocks[:-1, -1].astype(jnp.int32)])

    def first_pass(packed):
        inputs, cot_rows, decays, writes, reads, doc_row, prev_doc = packed
        weights, read_w, write_w, block_gain = mixer_block_pieces(decays, writes, reads, doc_row, prev_doc)
        block_state = jnp.einsum('shp,hsn->hpn', inputs.astype(jnp.float32), write_w.astype(jnp.float32))
        block_back = jnp.einsum('thp,htn->hpn', cot_rows.astype(jnp.float32), read_w.astype(jnp.float32))
        return (block_gain, block_state, block_back)
    block_gains, block_states, block_backs = lax.map(first_pass, (input_blocks, cot_blocks, decay_blocks, write_blocks, read_blocks, doc_blocks, prev_docs))

    def forward_step(running_sum, pair_in):
        return (pair_in[0][:, None, None] * running_sum + pair_in[1], running_sum)

    def backward_step(running_sum, pair_in):
        return (pair_in[1] + pair_in[0][:, None, None] * running_sum, running_sum)
    start_zero = jnp.zeros((MIXER_HEADS, SP, SN), jnp.float32)
    _, carry_in = lax.scan(forward_step, start_zero, (block_gains, block_states))
    _, carry_out = lax.scan(backward_step, start_zero, (block_gains, block_backs), reverse=True)

    def second_pass(packed):
        inputs, cot_rows, decays, writes, reads, doc_row, prev_doc, state_in, state_out = packed
        weights, read_w, write_w, block_gain = mixer_block_pieces(decays, writes, reads, doc_row, prev_doc)
        weight_f32 = weights.astype(jnp.float32)
        mixed_out = jnp.einsum('hts,shp->thp', weight_f32, inputs.astype(jnp.float32))
        mixed_out = mixed_out + jnp.einsum('hpn,htn->thp', state_in, read_w.astype(jnp.float32), precision=lax.Precision.HIGHEST)
        grad_rows = jnp.einsum('hts,thp->shp', weight_f32, cot_rows.astype(jnp.float32))
        grad_rows = grad_rows + jnp.einsum('hpn,hsn->shp', state_out, write_w.astype(jnp.float32), precision=lax.Precision.HIGHEST)
        return (mixed_out.astype(jnp.bfloat16), grad_rows.astype(jnp.bfloat16))
    mixed_all, grad_all = lax.map(second_pass, (input_blocks, cot_blocks, decay_blocks, write_blocks, read_blocks, doc_blocks, prev_docs, carry_in, carry_out))
    return (mixed_all.reshape(PACKED_TOKENS, MIXER_HEADS * SP), grad_all.reshape(PACKED_TOKENS, MIXER_HEADS * SP))

def attention_reference(query_head_matrix, key_head_matrix, value_head_matrix, document_ids, attention_output_gradient):
    queries_per_group = QUERY_HEADS // KEY_VALUE_HEADS
    inv_root = 1.0 / math.sqrt(HEAD_CHANNELS)
    leading_rows = SPAN * TOK_DEV
    attention_span = (SPAN + 1) * TOK_DEV
    query_rows_all = query_head_matrix.reshape(PACKED_TOKENS, KEY_VALUE_HEADS, queries_per_group, HEAD_CHANNELS)
    output_gradient_all = attention_output_gradient.reshape(PACKED_TOKENS, KEY_VALUE_HEADS, queries_per_group, HEAD_CHANNELS)
    padded_keys = jnp.concatenate([jnp.zeros((leading_rows, KEY_VALUE_HEADS * HEAD_CHANNELS), key_head_matrix.dtype), key_head_matrix], axis=0)
    padded_values = jnp.concatenate([jnp.zeros((leading_rows, KEY_VALUE_HEADS * HEAD_CHANNELS), value_head_matrix.dtype), value_head_matrix], axis=0)
    doc_pad = jnp.concatenate([jnp.full((leading_rows,), -1, jnp.int32), document_ids.astype(jnp.int32)])

    def attend_block(running_sums, block_no):
        key_sums, value_sums = running_sums
        starting_row = (block_no * TOK_DEV).astype(jnp.int32)
        query_block_rows = lax.dynamic_slice_in_dim(query_rows_all, starting_row, TOK_DEV, 0).astype(jnp.float32)
        output_gradient_block = lax.dynamic_slice_in_dim(output_gradient_all, starting_row, TOK_DEV, 0).astype(jnp.float32)
        key_span_rows = lax.dynamic_slice_in_dim(padded_keys, starting_row, attention_span, 0).reshape(attention_span, KEY_VALUE_HEADS, HEAD_CHANNELS).astype(jnp.float32)
        value_span_rows = lax.dynamic_slice_in_dim(padded_values, starting_row, attention_span, 0).reshape(attention_span, KEY_VALUE_HEADS, HEAD_CHANNELS).astype(jnp.float32)
        doc_win = lax.dynamic_slice_in_dim(doc_pad, starting_row, attention_span, 0)
        doc_query = lax.dynamic_slice_in_dim(document_ids.astype(jnp.int32), starting_row, TOK_DEV, 0)
        key_pos = starting_row - leading_rows + jnp.arange(attention_span, dtype=jnp.int32)
        query_pos = starting_row + jnp.arange(TOK_DEV, dtype=jnp.int32)
        inside = (doc_win[None, :] == doc_query[:, None]) & (key_pos[None, :] <= query_pos[:, None])
        scores = jnp.einsum('tgid,sgd->gits', query_block_rows, key_span_rows) * inv_root
        scores = jnp.where(inside[None, None], scores, -jnp.inf)
        row_peak = lax.optimization_barrier(jnp.max(scores, axis=-1, keepdims=True))
        raised = jnp.exp(scores - row_peak)
        prob_mat = lax.optimization_barrier((raised / lax.optimization_barrier(jnp.sum(raised, axis=-1, keepdims=True))).astype(jnp.bfloat16))
        probability_single = prob_mat.astype(jnp.float32)
        out_block = jnp.einsum('gits,sgd->tgid', probability_single, value_span_rows).astype(jnp.bfloat16)
        prob_grad = jnp.einsum('tgid,sgd->gits', output_gradient_block, value_span_rows)
        inner_sum = lax.optimization_barrier(jnp.sum(probability_single * prob_grad, axis=-1, keepdims=True))
        score_gradient = lax.optimization_barrier((probability_single * (prob_grad - inner_sum) * inv_root).astype(jnp.bfloat16))
        key_gradient = jnp.einsum('wpza,zwpo->awo', score_gradient.astype(jnp.float32), query_block_rows).reshape(attention_span, KEY_VALUE_HEADS * HEAD_CHANNELS)
        value_gradient = jnp.einsum('wpza,zwpo->awo', probability_single, output_gradient_block).reshape(attention_span, KEY_VALUE_HEADS * HEAD_CHANNELS)
        key_sums = lax.dynamic_update_slice_in_dim(key_sums, lax.dynamic_slice_in_dim(key_sums, starting_row, attention_span, 0) + key_gradient, starting_row, 0)
        value_sums = lax.dynamic_update_slice_in_dim(value_sums, lax.dynamic_slice_in_dim(value_sums, starting_row, attention_span, 0) + value_gradient, starting_row, 0)
        return ((key_sums, value_sums), out_block.reshape(TOK_DEV, QUERY_HEADS * HEAD_CHANNELS))
    initial_sums = jnp.zeros((leading_rows + PACKED_TOKENS, KEY_VALUE_HEADS * HEAD_CHANNELS), jnp.float32)
    final_sums, out_blocks = lax.scan(attend_block, (initial_sums, initial_sums), jnp.arange(N_CTX, dtype=jnp.int32))
    attention_out = out_blocks.reshape(PACKED_TOKENS, QUERY_HEADS * HEAD_CHANNELS)
    grad_key = final_sums[0][leading_rows:].astype(jnp.bfloat16)
    grad_value = final_sums[1][leading_rows:].astype(jnp.bfloat16)
    return (attention_out, grad_key, grad_value)

def reference(query_head_matrix, key_head_matrix, value_head_matrix, ssm_input, log_decay, state_write, state_read, document_ids, attention_output_gradient, cot_mixer):
    attention_out, grad_key, grad_value = attention_reference(query_head_matrix, key_head_matrix, value_head_matrix, document_ids, attention_output_gradient)
    mixer_out, grad_input = mixer_reference(ssm_input, log_decay, state_write, state_read, document_ids, cot_mixer)
    return (attention_out, mixer_out, grad_key, grad_value, grad_input)
```

```python
import functools
import math

import jax
import jax.numpy as jnp
from jax import lax
from jax.experimental import pallas as pl
from jax.experimental.pallas import tpu as pltpu
from jax.sharding import PartitionSpec as P

HEAD_CHANNELS = 128
BF16 = jnp.bfloat16
F32 = jnp.float32
NT = (((1,), (1,)), ((), ()))
TN = (((0,), (0,)), ((), ()))


def passed_along(block, axis, distance):
    devices = range(lax.axis_size(axis))
    route = [(i - distance, i) for i in devices if i - distance in devices]
    return lax.ppermute(block, axis, route)


def dot(a, b, dims=(((1,), (0,)), ((), ()))):
    return lax.dot_general(a, b, dims, preferred_element_type=F32)


def iota(shape, dim):
    return lax.broadcasted_iota(jnp.int32, shape, dim)


def split3(v):
    hi = v.astype(BF16)
    rest = v - hi.astype(F32)
    mid = rest.astype(BF16)
    lo = (rest - mid.astype(F32)).astype(BF16)
    return hi, mid, lo


def aux_parts(aux, heads):
    wide = aux.astype(F32)
    lam = wide[:, :heads] + wide[:, heads : 2 * heads] + wide[:, 2 * heads : 3 * heads]
    return lam, wide[:, 3 * heads : 4 * heads]


def pack_kernel(heads, key_ref, value_ref, write_ref, read_ref, decay_ref, doc_ref, m_ref, n_ref):
    tokens = key_ref.shape[0]
    kv = key_ref.shape[1]
    tri = jnp.where(
        iota((tokens, tokens), 0) >= iota((tokens, tokens), 1), 1.0, 0.0
    ).astype(BF16)
    lam = sum(dot(tri, part) for part in split3(decay_ref[...]))
    docs = jnp.broadcast_to(doc_ref[...].astype(F32) + 1.0, (tokens, tokens)).T
    parts = [part.astype(F32) for part in split3(lam)] + [docs[:, :heads]]
    aux = jnp.concatenate(parts, axis=1).astype(BF16)
    state = write_ref.shape[1]
    m_ref[:, :kv] = key_ref[...]
    m_ref[:, kv : 2 * kv] = value_ref[...]
    m_ref[:, 2 * kv : 2 * kv + state] = write_ref[...]
    m_ref[:, 2 * kv + state :] = aux
    n_ref[:, :state] = read_ref[...]
    n_ref[:, state:] = aux


def attn_kernel(
    kv, docs_at, doc_ref, m0, m1, m2, q_ref, cot_ref, out_ref, own_ref, back1_ref, back2_ref
):
    tokens = m0.shape[0]
    group = q_ref.shape[1] // HEAD_CHANNELS
    inv_root = 1.0 / math.sqrt(HEAD_CHANNELS)
    width = HEAD_CHANNELS
    key_cols = pl.ds(pl.multiple_of(pl.program_id(0) * width, width), width)
    value_cols = pl.ds(pl.multiple_of(kv + pl.program_id(0) * width, width), width)
    tiles = (m2, m1, m0)
    keys = jnp.concatenate([tile[:, key_cols] for tile in tiles], axis=0)
    values = jnp.concatenate([tile[:, value_cols] for tile in tiles], axis=0)
    span = keys.shape[0]
    doc_s = jnp.concatenate(
        [tile[:, docs_at : docs_at + 1].astype(F32) for tile in tiles], axis=0
    )
    doc_t = doc_ref[...].astype(F32) + 1.0
    inside = (doc_s == doc_t) & (
        iota((span, tokens), 0) - (span - tokens) <= iota((span, tokens), 1)
    )
    inside = jnp.where(inside, 1.0, 0.0)
    inside = jnp.concatenate([inside] * group, axis=1) > 0.5
    query = jnp.concatenate(
        [q_ref[:, i * width : (i + 1) * width] for i in range(group)], axis=0
    )
    cot = jnp.concatenate(
        [cot_ref[:, i * width : (i + 1) * width] for i in range(group)], axis=0
    )
    score = jnp.where(inside, dot(keys, query, NT) * inv_root, -1e30)
    raised = jnp.exp(score - jnp.max(score, axis=0, keepdims=True))
    raised = jnp.where(inside, raised, 0.0)
    prob = (raised * (1.0 / jnp.sum(raised, axis=0, keepdims=True))).astype(BF16)
    out = dot(values, prob, TN).T
    for i in range(group):
        out_ref[:, i * width : (i + 1) * width] = out[i * tokens : (i + 1) * tokens].astype(BF16)
    prob_grad = dot(values, cot, NT)
    prob32 = prob.astype(F32)
    inner = jnp.sum(prob32 * prob_grad, axis=0, keepdims=True)
    score_grad = (prob32 * (prob_grad - inner) * inv_root).astype(BF16)
    key_grad = dot(score_grad, query)
    value_grad = dot(prob, cot)
    back2_ref[:, :width] = key_grad[:tokens].astype(BF16)
    back2_ref[:, width:] = value_grad[:tokens].astype(BF16)
    back1_ref[:, :width] = key_grad[tokens : 2 * tokens].astype(BF16)
    back1_ref[:, width:] = value_grad[tokens : 2 * tokens].astype(BF16)
    own_ref[:, :width] = key_grad[2 * tokens :]
    own_ref[:, width:] = value_grad[2 * tokens :]


def local_kernel(
    heads, head_width, write_at, doc_ref, m0, n0, x_ref, cot_ref, mixed_ref, grad_ref
):
    tokens = m0.shape[0]
    state = n0.shape[1] - 4 * heads
    cols = x_ref.shape[1]
    step_heads = cols // head_width
    lanes = 4 * heads
    aux = n0[:, state:]
    pick = (iota((lanes, lanes), 0) % heads) == (
        iota((lanes, lanes), 1) + pl.program_id(0) * step_heads
    )
    pick &= (iota((lanes, lanes), 0) < 3 * heads) & (iota((lanes, lanes), 1) < step_heads)
    lam = dot(aux, jnp.where(pick, 1.0, 0.0).astype(BF16))
    lam_t = lam.T
    doc_col = aux[:, 3 * heads : 3 * heads + 1].astype(F32)
    doc_row = doc_ref[...].astype(F32) + 1.0
    inside = (iota((tokens, tokens), 0) >= iota((tokens, tokens), 1)) & (doc_col == doc_row)
    score = dot(n0[:, :state], m0[:, write_at : write_at + state], NT)
    per = HEAD_CHANNELS // head_width
    lane_head = iota((tokens, HEAD_CHANNELS), 1) // head_width
    for pair in range(step_heads // per):
        at = slice(pair * HEAD_CHANNELS, (pair + 1) * HEAD_CHANNELS)
        x = x_ref[:, at]
        cot = cot_ref[:, at]
        mixed = grad = None
        for j in range(per):
            head = pair * per + j
            gap = lam[:, head : head + 1] - lam_t[head : head + 1, :]
            weights = (jnp.exp(jnp.where(inside, gap, -jnp.inf)) * score).astype(BF16)
            mixed_j = dot(weights, x)
            grad_j = dot(weights, cot, TN)
            mixed = mixed_j if j == 0 else jnp.where(lane_head == j, mixed_j, mixed)
            grad = grad_j if j == 0 else jnp.where(lane_head == j, grad_j, grad)
        mixed_ref[:, at] = mixed
        grad_ref[:, at] = grad


def final_kernel(
    heads,
    head_width,
    write_at,
    m0,
    m1,
    m2,
    n0,
    n1,
    n2,
    own_ref,
    r1_ref,
    r2_ref,
    x1_ref,
    x2_ref,
    c1_ref,
    c2_ref,
    mixed_ref,
    grad_ref,
    mixer_out_ref,
    grad_input_ref,
    grad_key_ref,
    grad_value_ref,
):
    tokens = m0.shape[0]
    state = n0.shape[1] - 4 * heads
    cols = x1_ref.shape[1]
    step_heads = cols // head_width

    @pl.when(pl.program_id(0) == 0)
    def _():
        total = own_ref[...] + r1_ref[...].astype(F32) + r2_ref[...].astype(F32)
        width = HEAD_CHANNELS
        for g in range(own_ref.shape[1] // (2 * width)):
            grad_key_ref[:, g * width : (g + 1) * width] = total[
                :, 2 * g * width : (2 * g + 1) * width
            ].astype(BF16)
            grad_value_ref[:, g * width : (g + 1) * width] = total[
                :, (2 * g + 1) * width : (2 * g + 2) * width
            ].astype(BF16)

    spread = (iota((heads, cols), 0) - pl.program_id(0) * step_heads) == (
        iota((heads, cols), 1) // head_width
    )
    spread = jnp.where(spread, 1.0, 0.0).astype(BF16)

    def widen(scale):
        return sum(dot(part, spread) for part in split3(scale))

    def same(a, b):
        return jnp.where(a == b, 1.0, 0.0)

    write_cols = slice(write_at, write_at + state)
    lam0, doc0 = aux_parts(n0[:, state:], heads)
    lam1, doc1 = aux_parts(m1[:, write_at + state :], heads)
    lam2, doc2 = aux_parts(m2[:, write_at + state :], heads)
    next1, next_doc1 = aux_parts(n1[:, state:], heads)
    next2, next_doc2 = aux_parts(n2[:, state:], heads)

    def last(v):
        return v[tokens - 1 : tokens]

    entry0 = jnp.exp(lam0) * same(doc0, last(doc1))
    exit1 = jnp.exp(last(lam1) - lam1) * same(doc1, last(doc1))
    gain1 = jnp.exp(last(lam1)) * same(last(doc1), last(doc2))
    exit2 = jnp.exp(last(lam2) - lam2) * same(doc2, last(doc2)) * gain1
    exit0 = jnp.exp(last(lam0) - lam0) * same(doc0, last(doc0))
    entry1 = jnp.exp(next1) * same(next_doc1, last(doc0))
    next_gain = jnp.exp(last(next1)) * same(last(next_doc1), last(doc0))
    entry2 = jnp.exp(next2) * same(next_doc2, last(next_doc1)) * next_gain

    read0 = n0[:, :state]
    write0 = m0[:, write_cols]
    score1 = dot(read0, m1[:, write_cols], NT).astype(BF16)
    score2 = dot(read0, m2[:, write_cols], NT).astype(BF16)
    back1 = dot(write0, n1[:, :state], NT).astype(BF16)
    back2 = dot(write0, n2[:, :state], NT).astype(BF16)

    def scaled(ref, scale):
        return (ref[...].astype(F32) * widen(scale)).astype(BF16)

    carried = dot(score1, scaled(x1_ref, exit1)) + dot(score2, scaled(x2_ref, exit2))
    mixer_out_ref[...] = (mixed_ref[...] + widen(entry0) * carried).astype(BF16)
    returned = dot(back1, scaled(c1_ref, entry1)) + dot(back2, scaled(c2_ref, entry2))
    grad_input_ref[...] = (grad_ref[...] + widen(exit0) * returned).astype(BF16)


def whole(shape):
    return pl.BlockSpec(shape, lambda i: (0, 0))


def columns(rows, cols):
    return pl.BlockSpec((rows, cols), lambda i: (0, i))


def shards(
    query_head_matrix,
    key_head_matrix,
    value_head_matrix,
    ssm_input,
    log_decay,
    state_write,
    state_read,
    document_ids,
    attention_output_gradient,
    cot_mixer,
):
    tokens, kv = key_head_matrix.shape
    kv_local = kv // HEAD_CHANNELS
    heads = log_decay.shape[1]
    state = state_write.shape[1]
    head_width = ssm_input.shape[1] // heads
    group_cols = query_head_matrix.shape[1] // kv_local
    write_at = 2 * kv
    doc_row = document_ids.reshape(1, tokens)
    aux = 4 * heads
    m_cols = 2 * kv + state + aux
    n_cols = state + aux
    step_cols = min(512, ssm_input.shape[1])
    steps = ssm_input.shape[1] // step_cols
    shape = jax.ShapeDtypeStruct
    params = pltpu.CompilerParams(vmem_limit_bytes=48 * 1024 * 1024)

    m0, n0 = pl.pallas_call(
        functools.partial(pack_kernel, heads),
        out_shape=(shape((tokens, m_cols), BF16), shape((tokens, n_cols), BF16)),
        compiler_params=params,
        name="pack",
    )(key_head_matrix, value_head_matrix, state_write, state_read, log_decay, doc_row)
    m1 = passed_along(m0, "ctx", 1)
    m2 = passed_along(m0, "ctx", 2)
    n1 = passed_along(n0, "ctx", -1)
    n2 = passed_along(n0, "ctx", -2)
    x1 = passed_along(ssm_input, "ctx", 1)
    c1 = passed_along(cot_mixer, "ctx", -1)
    x2 = passed_along(ssm_input, "ctx", 2)
    c2 = passed_along(cot_mixer, "ctx", -2)

    mixed, grad = pl.pallas_call(
        functools.partial(local_kernel, heads, head_width, write_at),
        grid=(steps,),
        in_specs=[
            whole((1, tokens)),
            whole((tokens, m_cols)),
            whole((tokens, n_cols)),
            columns(tokens, step_cols),
            columns(tokens, step_cols),
        ],
        out_specs=[columns(tokens, step_cols)] * 2,
        out_shape=(shape(ssm_input.shape, F32),) * 2,
        compiler_params=params,
        name="local_mixer",
    )(doc_row, m0, n0, ssm_input, cot_mixer)

    kv2 = 2 * HEAD_CHANNELS
    attention_out, own, back1, back2 = pl.pallas_call(
        functools.partial(attn_kernel, kv, 2 * kv + state + 3 * heads),
        grid=(kv_local,),
        in_specs=[whole((1, tokens))]
        + [whole((tokens, m_cols))] * 3
        + [columns(tokens, group_cols)] * 2,
        out_specs=[columns(tokens, group_cols)] + [columns(tokens, kv2)] * 3,
        out_shape=(
            shape(query_head_matrix.shape, BF16),
            shape((tokens, 2 * kv), F32),
            shape((tokens, 2 * kv), BF16),
            shape((tokens, 2 * kv), BF16),
        ),
        compiler_params=params,
        name="attention",
    )(doc_row, m0, m1, m2, query_head_matrix, attention_output_gradient)
    r1 = passed_along(back1, "ctx", -1)
    r2 = passed_along(back2, "ctx", -2)

    mixer_out, grad_input, grad_key, grad_value = pl.pallas_call(
        functools.partial(final_kernel, heads, head_width, write_at),
        grid=(steps,),
        in_specs=[whole((tokens, m_cols))] * 3
        + [whole((tokens, n_cols))] * 3
        + [whole((tokens, 2 * kv))] * 3
        + [columns(tokens, step_cols)] * 6,
        out_specs=[columns(tokens, step_cols)] * 2 + [whole((tokens, kv))] * 2,
        out_shape=(
            shape(ssm_input.shape, BF16),
            shape(cot_mixer.shape, BF16),
            shape(key_head_matrix.shape, BF16),
            shape(value_head_matrix.shape, BF16),
        ),
        compiler_params=params,
        name="final",
    )(m0, m1, m2, n0, n1, n2, own, r1, r2, x1, x2, c1, c2, mixed, grad)
    return (attention_out, mixer_out, grad_key, grad_value, grad_input)


def solution(mesh):
    return jax.shard_map(
        shards,
        mesh=mesh,
        in_specs=(
            P("ctx", "tp"),
            P("ctx", "tp"),
            P("ctx", "tp"),
            P("ctx", "tp"),
            P("ctx", "tp"),
            P("ctx", None),
            P("ctx", None),
            P("ctx"),
            P("ctx", "tp"),
            P("ctx", "tp"),
        ),
        out_specs=(P("ctx", "tp"), P("ctx", "tp"), P("ctx", "tp"), P("ctx", "tp"), P("ctx", "tp")),
        check_vma=False,
    )
```

```python
import functools
import math

import jax
import jax.numpy as jnp
from jax import lax
from jax.experimental import pallas as pl
from jax.experimental.pallas import tpu as pltpu
from jax.sharding import PartitionSpec as P

HEAD_CHANNELS = 128
BF16 = jnp.bfloat16
F32 = jnp.float32
VMEM_LIMIT = 32 * 1024 * 1024
PACK_LIMIT = 60 * 1024 * 1024
NT = (((1,), (1,)), ((), ()))
TN = (((0,), (0,)), ((), ()))


def passed_along(block, axis, distance):
    devices = range(lax.axis_size(axis))
    route = [(i - distance, i) for i in devices if i - distance in devices]
    return lax.ppermute(block, axis, route)


def dot(a, b, dims=(((1,), (0,)), ((), ()))):
    return lax.dot_general(a, b, dims, preferred_element_type=F32)


def iota(shape, dim):
    return lax.broadcasted_iota(jnp.int32, shape, dim)


def split3(v):
    hi = v.astype(BF16)
    rest = v - hi.astype(F32)
    mid = rest.astype(BF16)
    lo = (rest - mid.astype(F32)).astype(BF16)
    return hi, mid, lo


def cumulative(decay_t):
    tokens = decay_t.shape[1]
    tri = iota((tokens, tokens), 0) >= iota((tokens, tokens), 1)
    tri = jnp.where(tri, 1.0, 0.0).astype(BF16)
    return sum(dot(tri, part, NT) for part in split3(decay_t))


def thirds(v):
    return jnp.concatenate([part.astype(F32) for part in split3(v)], axis=1).astype(BF16)


def spread(heads, head_width, low, cols):
    offset = iota((heads, cols), 1) + low - iota((heads, cols), 0) * head_width
    match = jnp.where((offset >= 0) & (offset < head_width), 1.0, 0.0)
    return jnp.concatenate([match] * 3, axis=0).astype(BF16)


def aux_parts(aux, heads):
    wide = aux.astype(F32)
    lam = wide[:, :heads] + wide[:, heads : 2 * heads] + wide[:, 2 * heads : 3 * heads]
    return lam, wide[:, 3 * heads : 4 * heads]


def pack_kernel(key_ref, value_ref, write_ref, decay_ref, doc_ref, m_ref):
    tokens, kv = key_ref.shape
    heads = decay_ref.shape[0]
    state = write_ref.shape[1]
    lam = cumulative(decay_ref[...])
    docs = jnp.broadcast_to(doc_ref[...].astype(F32) + 1.0, (tokens, tokens)).T[:, :heads]
    aux = jnp.concatenate([p.astype(F32) for p in split3(lam)] + [docs], axis=1).astype(BF16)
    m_ref[:, :kv] = key_ref[...]
    m_ref[:, kv : 2 * kv] = value_ref[...]
    m_ref[:, 2 * kv : 2 * kv + state] = write_ref[...]
    m_ref[:, 2 * kv + state :] = aux


def attn_kernel(
    kv,
    docs_at,
    doc_ref,
    read_ref,
    m0,
    m1,
    m2,
    q_ref,
    cot_ref,
    out_ref,
    own_ref,
    back1_ref,
    back2_ref,
):
    tokens = m0.shape[0]
    group = q_ref.shape[1] // HEAD_CHANNELS
    inv_root = 1.0 / math.sqrt(HEAD_CHANNELS)
    width = HEAD_CHANNELS
    tiles = (m2, m1, m0)
    key_cols = pl.ds(pl.multiple_of(pl.program_id(0) * width, width), width)
    value_cols = pl.ds(pl.multiple_of(kv + pl.program_id(0) * width, width), width)
    keys = jnp.concatenate([tile[:, key_cols] for tile in tiles], axis=0)
    values = jnp.concatenate([tile[:, value_cols] for tile in tiles], axis=0)
    span = keys.shape[0]
    doc_s = jnp.concatenate(
        [tile[:, docs_at : docs_at + 1].astype(F32) for tile in tiles], axis=0
    )
    doc_t = doc_ref[...].astype(F32) + 1.0
    inside = (doc_s == doc_t) & (
        iota((span, tokens), 0) - (span - tokens) <= iota((span, tokens), 1)
    )
    inside = jnp.where(inside, 1.0, 0.0)
    inside = jnp.concatenate([inside] * group, axis=1) > 0.5
    query = jnp.concatenate(
        [q_ref[:, i * width : (i + 1) * width] for i in range(group)], axis=0
    )
    cot = jnp.concatenate(
        [cot_ref[:, i * width : (i + 1) * width] for i in range(group)], axis=0
    )
    score = jnp.where(inside, dot(keys, query, NT) * inv_root, -1e30)
    raised = jnp.exp(score - jnp.max(score, axis=0, keepdims=True))
    raised = jnp.where(inside, raised, 0.0)
    prob = (raised * (1.0 / jnp.sum(raised, axis=0, keepdims=True))).astype(BF16)
    out = dot(values, prob, TN).T
    for i in range(group):
        out_ref[:, i * width : (i + 1) * width] = out[i * tokens : (i + 1) * tokens].astype(BF16)
    prob_grad = dot(values, cot, NT)
    prob32 = prob.astype(F32)
    inner = jnp.sum(prob32 * prob_grad, axis=0, keepdims=True)
    score_grad = (prob32 * (prob_grad - inner) * inv_root).astype(BF16)
    key_grad = dot(score_grad, query)
    value_grad = dot(prob, cot)
    low = pl.multiple_of(pl.program_id(0) * 2 * width, 2 * width)
    key_at = pl.ds(low, width)
    value_at = pl.ds(pl.multiple_of(low + width, width), width)
    back2_ref[:, key_at] = key_grad[:tokens].astype(BF16)
    back2_ref[:, value_at] = value_grad[:tokens].astype(BF16)
    back1_ref[:, key_at] = key_grad[tokens : 2 * tokens].astype(BF16)
    back1_ref[:, value_at] = value_grad[tokens : 2 * tokens].astype(BF16)
    own_ref[:, key_at] = key_grad[2 * tokens :]
    own_ref[:, value_at] = value_grad[2 * tokens :]

    @pl.when(pl.program_id(0) == 0)
    def _():
        state = read_ref.shape[1]
        aux = m0[:, 2 * kv + state :]
        for back_ref in (back1_ref, back2_ref):
            back_ref[:, 2 * kv : 2 * kv + state] = read_ref[...]
            back_ref[:, 2 * kv + state :] = aux


def local_kernel(
    head_width, doc_ref, write_ref, read_ref, decay_ref, x_ref, cot_ref, mixed_ref, grad_ref
):
    tokens, cols = x_ref.shape
    step_heads = cols // head_width
    lam = cumulative(decay_ref[...])
    upper = iota((tokens, tokens), 0) <= iota((tokens, tokens), 1)
    upper = jnp.where(upper, 1.0, 0.0).astype(BF16)
    lam_t = sum(dot(part, upper) for part in split3(decay_ref[...]))
    doc_row = doc_ref[...].astype(F32)
    doc_col = jnp.broadcast_to(doc_row, (tokens, tokens)).T
    inside = (iota((tokens, tokens), 0) >= iota((tokens, tokens), 1)) & (doc_col == doc_row)
    score = dot(read_ref[...], write_ref[...], NT)
    per = HEAD_CHANNELS // head_width
    lane_head = iota((tokens, HEAD_CHANNELS), 1) // head_width
    for pair in range(step_heads // per):
        at = slice(pair * HEAD_CHANNELS, (pair + 1) * HEAD_CHANNELS)
        x = x_ref[:, at]
        cot = cot_ref[:, at]
        mixed = grad = None
        for j in range(per):
            head = pair * per + j
            gap = lam[:, head : head + 1] - lam_t[head : head + 1, :]
            weights = (jnp.exp(jnp.where(inside, gap, -jnp.inf)) * score).astype(BF16)
            mixed_j = dot(weights, x)
            grad_j = dot(weights, cot, TN)
            mixed = mixed_j if j == 0 else jnp.where(lane_head == j, mixed_j, mixed)
            grad = grad_j if j == 0 else jnp.where(lane_head == j, grad_j, grad)
        mixed_ref[:, at] = mixed
        grad_ref[:, at] = grad


def same(a, b):
    return jnp.where(a == b, 1.0, 0.0)


def carried_kernel(
    head_width,
    decay_ref,
    doc_ref,
    read_ref,
    write1_ref,
    aux1_ref,
    write2_ref,
    aux2_ref,
    x1_ref,
    x2_ref,
    mixed_ref,
    out_ref,
):
    tokens, cols = x1_ref.shape
    heads = decay_ref.shape[0]
    lam = cumulative(decay_ref[...])
    docs = jnp.broadcast_to(doc_ref[...].astype(F32) + 1.0, (tokens, tokens)).T[:, :heads]
    lam1, doc1 = aux_parts(aux1_ref[...], heads)
    lam2, doc2 = aux_parts(aux2_ref[...], heads)

    def last(v):
        return v[tokens - 1 :]

    entry = thirds(jnp.exp(lam) * same(docs, last(doc1)))
    gain = jnp.exp(last(lam1)) * same(last(doc1), last(doc2))
    exit1 = thirds(jnp.exp(last(lam1) - lam1) * same(doc1, last(doc1)))
    exit2 = thirds(jnp.exp(last(lam2) - lam2) * same(doc2, last(doc2)) * gain)
    score1 = dot(read_ref[...], write1_ref[...], NT).astype(BF16)
    score2 = dot(read_ref[...], write2_ref[...], NT).astype(BF16)
    step = min(cols, 512)
    for low in range(0, cols, step):
        at = slice(low, low + step)
        to_cols = spread(heads, head_width, low, step)
        x1 = (x1_ref[:, at].astype(F32) * dot(exit1, to_cols)).astype(BF16)
        x2 = (x2_ref[:, at].astype(F32) * dot(exit2, to_cols)).astype(BF16)
        carried = (dot(score1, x1) + dot(score2, x2)) * dot(entry, to_cols)
        out_ref[:, at] = (mixed_ref[:, at] + carried).astype(BF16)


def returned_kernel(
    head_width,
    decay_ref,
    doc_ref,
    write_ref,
    r1_ref,
    r2_ref,
    own_ref,
    c1_ref,
    c2_ref,
    grad_ref,
    out_ref,
    grad_key_ref,
    grad_value_ref,
):
    tokens, cols = c1_ref.shape
    heads = decay_ref.shape[0]
    state = write_ref.shape[1]
    width = HEAD_CHANNELS
    kv2 = own_ref.shape[1]
    total = own_ref[...] + r1_ref[:, :kv2].astype(F32) + r2_ref[:, :kv2].astype(F32)
    for g in range(kv2 // (2 * width)):
        at = slice(g * width, (g + 1) * width)
        low = 2 * g * width
        grad_key_ref[:, at] = total[:, low : low + width].astype(BF16)
        grad_value_ref[:, at] = total[:, low + width : low + 2 * width].astype(BF16)

    def last(v):
        return v[tokens - 1 :]

    lam = cumulative(decay_ref[...])
    docs = jnp.broadcast_to(doc_ref[...].astype(F32) + 1.0, (tokens, tokens)).T[:, :heads]
    lam1, doc1 = aux_parts(r1_ref[:, kv2 + state :], heads)
    lam2, doc2 = aux_parts(r2_ref[:, kv2 + state :], heads)
    exit_w = thirds(jnp.exp(last(lam) - lam) * same(docs, last(docs)))
    gain = jnp.exp(last(lam1)) * same(last(doc1), last(docs))
    entry1 = thirds(jnp.exp(lam1) * same(doc1, last(docs)))
    entry2 = thirds(jnp.exp(lam2) * same(doc2, last(doc1)) * gain)
    score1 = dot(write_ref[...], r1_ref[:, kv2 : kv2 + state], NT).astype(BF16)
    score2 = dot(write_ref[...], r2_ref[:, kv2 : kv2 + state], NT).astype(BF16)
    step = min(cols, 512)
    for low in range(0, cols, step):
        at = slice(low, low + step)
        to_cols = spread(heads, head_width, low, step)
        c1 = (c1_ref[:, at].astype(F32) * dot(entry1, to_cols)).astype(BF16)
        c2 = (c2_ref[:, at].astype(F32) * dot(entry2, to_cols)).astype(BF16)
        returned = (dot(score1, c1) + dot(score2, c2)) * dot(exit_w, to_cols)
        out_ref[:, at] = (grad_ref[:, at] + returned).astype(BF16)


def whole(shape):
    return pl.BlockSpec(shape, lambda i: (0, 0))


def columns(rows, cols):
    return pl.BlockSpec((rows, cols), lambda i: (0, i))


def part(rows, width, low):
    return pl.BlockSpec((rows, width), lambda i: (0, low // width))


def shards(
    query_head_matrix,
    key_head_matrix,
    value_head_matrix,
    ssm_input,
    log_decay,
    state_write,
    state_read,
    document_ids,
    attention_output_gradient,
    cot_mixer,
):
    tokens, kv = key_head_matrix.shape
    kv_local = kv // HEAD_CHANNELS
    heads = log_decay.shape[1]
    state = state_write.shape[1]
    cols = ssm_input.shape[1]
    head_width = cols // heads
    group_cols = query_head_matrix.shape[1] // kv_local
    doc_row = document_ids.reshape(1, tokens)
    decay_t = log_decay.T
    aux = 4 * heads
    m_cols = 2 * kv + state + aux
    step_cols = min(512, cols)
    steps = cols // step_cols
    shape = jax.ShapeDtypeStruct
    params = pltpu.CompilerParams(vmem_limit_bytes=VMEM_LIMIT)

    x1 = passed_along(ssm_input, "ctx", 1)
    c2 = passed_along(cot_mixer, "ctx", -2)
    m0 = pl.pallas_call(
        pack_kernel,
        out_shape=shape((tokens, m_cols), BF16),
        compiler_params=pltpu.CompilerParams(vmem_limit_bytes=PACK_LIMIT),
        name="pack",
    )(key_head_matrix, value_head_matrix, state_write, decay_t, doc_row)
    m1 = passed_along(m0, "ctx", 1)
    m2 = passed_along(m0, "ctx", 2)
    c1 = passed_along(cot_mixer, "ctx", -1)
    decay_local, m1, m2 = lax.optimization_barrier((decay_t, m1, m2))
    mixed, grad = pl.pallas_call(
        functools.partial(local_kernel, head_width),
        grid=(steps,),
        in_specs=[
            whole((1, tokens)),
            whole((tokens, state)),
            whole((tokens, state)),
            pl.BlockSpec((heads // steps, tokens), lambda i: (i, 0)),
            columns(tokens, step_cols),
            columns(tokens, step_cols),
        ],
        out_specs=[columns(tokens, step_cols)] * 2,
        out_shape=(shape(ssm_input.shape, F32),) * 2,
        compiler_params=params,
        name="local_mixer",
    )(doc_row, state_write, state_read, decay_local, ssm_input, cot_mixer)

    mixed, grad, x0 = lax.optimization_barrier((mixed, grad, ssm_input))
    x2 = passed_along(x0, "ctx", 2)
    attention_out, own, back1, back2 = pl.pallas_call(
        functools.partial(attn_kernel, kv, 2 * kv + state + 3 * heads),
        grid=(kv_local,),
        in_specs=[whole((1, tokens)), whole((tokens, state))]
        + [whole((tokens, m_cols))] * 3
        + [columns(tokens, group_cols)] * 2,
        out_specs=[columns(tokens, group_cols), whole((tokens, 2 * kv))]
        + [whole((tokens, m_cols))] * 2,
        out_shape=(
            shape(query_head_matrix.shape, BF16),
            shape((tokens, 2 * kv), F32),
            shape((tokens, m_cols), BF16),
            shape((tokens, m_cols), BF16),
        ),
        compiler_params=params,
        name="attention",
    )(doc_row, state_read, m0, m1, m2, query_head_matrix, attention_output_gradient)
    r1 = passed_along(back1, "ctx", -1)
    back2, c1 = lax.optimization_barrier((back2, c1))
    r2 = passed_along(back2, "ctx", -2)


    write_at = 2 * kv
    mixer_out = pl.pallas_call(
        functools.partial(carried_kernel, head_width),
        grid=(1,),
        in_specs=[
            whole((heads, tokens)),
            whole((1, tokens)),
            whole((tokens, state)),
            part(tokens, state, write_at),
            part(tokens, aux, write_at + state),
            part(tokens, state, write_at),
            part(tokens, aux, write_at + state),
            whole((tokens, cols)),
            whole((tokens, cols)),
            whole((tokens, cols)),
        ],
        out_specs=whole((tokens, cols)),
        out_shape=shape(ssm_input.shape, BF16),
        compiler_params=params,
        name="carried",
    )(decay_t, doc_row, state_read, m1, m1, m2, m2, x1, x2, mixed)

    own, mixer_out = lax.optimization_barrier((own, mixer_out))
    grad_input, grad_key, grad_value = pl.pallas_call(
        functools.partial(returned_kernel, head_width),
        grid=(1,),
        in_specs=[
            whole((heads, tokens)),
            whole((1, tokens)),
            whole((tokens, state)),
            whole((tokens, m_cols)),
            whole((tokens, m_cols)),
            whole((tokens, 2 * kv)),
            whole((tokens, cols)),
            whole((tokens, cols)),
            whole((tokens, cols)),
        ],
        out_specs=[whole((tokens, cols))] + [whole((tokens, kv))] * 2,
        out_shape=(
            shape(cot_mixer.shape, BF16),
            shape(key_head_matrix.shape, BF16),
            shape(value_head_matrix.shape, BF16),
        ),
        compiler_params=params,
        name="returned",
    )(decay_t, doc_row, state_write, r1, r2, own, c1, c2, grad)
    return (attention_out, mixer_out, grad_key, grad_value, grad_input)


def solution(mesh):
    return jax.shard_map(
        shards,
        mesh=mesh,
        in_specs=(
            P("ctx", "tp"),
            P("ctx", "tp"),
            P("ctx", "tp"),
            P("ctx", "tp"),
            P("ctx", "tp"),
            P("ctx", None),
            P("ctx", None),
            P("ctx"),
            P("ctx", "tp"),
            P("ctx", "tp"),
        ),
        out_specs=(P("ctx", "tp"), P("ctx", "tp"), P("ctx", "tp"), P("ctx", "tp"), P("ctx", "tp")),
        check_vma=False,
    )
```

```python
import functools
import math

import jax
import jax.numpy as jnp
from jax import lax
from jax.experimental import pallas as pl
from jax.experimental.pallas import tpu as pltpu
from jax.sharding import PartitionSpec as P

HEAD_CHANNELS = 128
BF16 = jnp.bfloat16
F32 = jnp.float32
VMEM_LIMIT = 32 * 1024 * 1024
PACK_LIMIT = 60 * 1024 * 1024
NT = (((1,), (1,)), ((), ()))
TN = (((0,), (0,)), ((), ()))


def passed_along(block, axis, distance):
    devices = range(lax.axis_size(axis))
    route = [(i - distance, i) for i in devices if i - distance in devices]
    return lax.ppermute(block, axis, route)


def exchanged(block, axis, first):
    count = lax.axis_size(axis)
    route = []
    for i in range(first, count - 1, 2):
        route += [(i, i + 1), (i + 1, i)]
    return lax.ppermute(block, axis, route)


def dot(a, b, dims=(((1,), (0,)), ((), ()))):
    return lax.dot_general(a, b, dims, preferred_element_type=F32)


def iota(shape, dim):
    return lax.broadcasted_iota(jnp.int32, shape, dim)


def split3(v):
    hi = v.astype(BF16)
    rest = v - hi.astype(F32)
    mid = rest.astype(BF16)
    lo = (rest - mid.astype(F32)).astype(BF16)
    return hi, mid, lo


def cumulative(decay_t):
    tokens = decay_t.shape[1]
    tri = iota((tokens, tokens), 0) >= iota((tokens, tokens), 1)
    tri = jnp.where(tri, 1.0, 0.0).astype(BF16)
    return sum(dot(tri, part, NT) for part in split3(decay_t))


def thirds(v):
    return jnp.concatenate([part.astype(F32) for part in split3(v)], axis=1).astype(BF16)


def spread(heads, head_width, low, cols):
    offset = iota((heads, cols), 1) + low - iota((heads, cols), 0) * head_width
    match = jnp.where((offset >= 0) & (offset < head_width), 1.0, 0.0)
    return jnp.concatenate([match] * 3, axis=0).astype(BF16)


def aux_parts(aux, heads):
    wide = aux.astype(F32)
    lam = wide[:, :heads] + wide[:, heads : 2 * heads] + wide[:, 2 * heads : 3 * heads]
    return lam, wide[:, 3 * heads : 4 * heads]


def pack_kernel(
    key_ref, value_ref, write_ref, read_ref, decay_ref, doc_ref, m_ref, n_ref
):
    tokens, kv = key_ref.shape
    heads = decay_ref.shape[0]
    state = write_ref.shape[1]
    lam = cumulative(decay_ref[...])
    docs = jnp.broadcast_to(doc_ref[...].astype(F32) + 1.0, (tokens, tokens)).T[:, :heads]
    aux = jnp.concatenate([p.astype(F32) for p in split3(lam)] + [docs], axis=1).astype(BF16)
    m_ref[:, :kv] = key_ref[...]
    m_ref[:, kv : 2 * kv] = value_ref[...]
    m_ref[:, 2 * kv : 2 * kv + state] = write_ref[...]
    m_ref[:, 2 * kv + state :] = aux
    n_ref[:, :state] = read_ref[...]
    n_ref[:, state:] = jnp.zeros((tokens, n_ref.shape[1] - state), BF16)


def attn_kernel(
    kv,
    docs_at,
    doc_ref,
    read_ref,
    m0,
    m1,
    m2,
    q_ref,
    cot_ref,
    far_ref,
    out_ref,
    own_ref,
    back1_ref,
    back2_ref,
):
    tokens = m0.shape[0]
    group = q_ref.shape[1] // HEAD_CHANNELS
    inv_root = 1.0 / math.sqrt(HEAD_CHANNELS)
    width = HEAD_CHANNELS
    tiles = (m2, m1, m0)
    key_cols = pl.ds(pl.multiple_of(pl.program_id(0) * width, width), width)
    value_cols = pl.ds(pl.multiple_of(kv + pl.program_id(0) * width, width), width)
    keys = jnp.concatenate([tile[:, key_cols] for tile in tiles], axis=0)
    values = jnp.concatenate([tile[:, value_cols] for tile in tiles], axis=0)
    span = keys.shape[0]
    doc_s = jnp.concatenate(
        [tile[:, docs_at : docs_at + 1].astype(F32) for tile in tiles], axis=0
    )
    doc_t = doc_ref[...].astype(F32) + 1.0
    inside = (doc_s == doc_t) & (
        iota((span, tokens), 0) - (span - tokens) <= iota((span, tokens), 1)
    )
    inside = jnp.where(inside, 1.0, 0.0)
    inside = jnp.concatenate([inside] * group, axis=1) > 0.5
    query = jnp.concatenate(
        [q_ref[:, i * width : (i + 1) * width] for i in range(group)], axis=0
    )
    cot = jnp.concatenate(
        [cot_ref[:, i * width : (i + 1) * width] for i in range(group)], axis=0
    )
    score = jnp.where(inside, dot(keys, query, NT) * inv_root, -1e30)
    raised = jnp.exp(score - jnp.max(score, axis=0, keepdims=True))
    raised = jnp.where(inside, raised, 0.0)
    prob = (raised * (1.0 / jnp.sum(raised, axis=0, keepdims=True))).astype(BF16)
    out = dot(values, prob, TN).T
    for i in range(group):
        out_ref[:, i * width : (i + 1) * width] = out[i * tokens : (i + 1) * tokens].astype(BF16)
    prob_grad = dot(values, cot, NT)
    prob32 = prob.astype(F32)
    inner = jnp.sum(prob32 * prob_grad, axis=0, keepdims=True)
    score_grad = (prob32 * (prob_grad - inner) * inv_root).astype(BF16)
    key_grad = dot(score_grad, query)
    value_grad = dot(prob, cot)
    low = pl.multiple_of(pl.program_id(0) * 2 * width, 2 * width)
    key_at = pl.ds(low, width)
    value_at = pl.ds(pl.multiple_of(low + width, width), width)
    back2_ref[:, key_at] = key_grad[:tokens].astype(BF16)
    back2_ref[:, value_at] = value_grad[:tokens].astype(BF16)
    back1_ref[:, key_at] = key_grad[tokens : 2 * tokens].astype(BF16)
    back1_ref[:, value_at] = value_grad[tokens : 2 * tokens].astype(BF16)
    own_ref[:, key_at] = key_grad[2 * tokens :]
    own_ref[:, value_at] = value_grad[2 * tokens :]

    @pl.when(pl.program_id(0) == 0)
    def _():
        state = read_ref.shape[1]
        back1_ref[:, 2 * kv : 2 * kv + state] = read_ref[...]
        back1_ref[:, 2 * kv + state :] = m0[:, 2 * kv + state :]
        back2_ref[:, 2 * kv :] = far_ref[...]


def local_kernel(
    head_width, doc_ref, write_ref, read_ref, decay_ref, x_ref, cot_ref, mixed_ref, grad_ref
):
    tokens, cols = x_ref.shape
    step_heads = cols // head_width
    lam = cumulative(decay_ref[...])
    upper = iota((tokens, tokens), 0) <= iota((tokens, tokens), 1)
    upper = jnp.where(upper, 1.0, 0.0).astype(BF16)
    lam_t = sum(dot(part, upper) for part in split3(decay_ref[...]))
    doc_row = doc_ref[...].astype(F32)
    doc_col = jnp.broadcast_to(doc_row, (tokens, tokens)).T
    inside = (iota((tokens, tokens), 0) >= iota((tokens, tokens), 1)) & (doc_col == doc_row)
    score = dot(read_ref[...], write_ref[...], NT)
    per = HEAD_CHANNELS // head_width
    lane_head = iota((tokens, HEAD_CHANNELS), 1) // head_width
    for pair in range(step_heads // per):
        at = slice(pair * HEAD_CHANNELS, (pair + 1) * HEAD_CHANNELS)
        x = x_ref[:, at]
        cot = cot_ref[:, at]
        mixed = grad = None
        for j in range(per):
            head = pair * per + j
            gap = lam[:, head : head + 1] - lam_t[head : head + 1, :]
            weights = (jnp.exp(jnp.where(inside, gap, -jnp.inf)) * score).astype(BF16)
            mixed_j = dot(weights, x)
            grad_j = dot(weights, cot, TN)
            mixed = mixed_j if j == 0 else jnp.where(lane_head == j, mixed_j, mixed)
            grad = grad_j if j == 0 else jnp.where(lane_head == j, grad_j, grad)
        mixed_ref[:, at] = mixed
        grad_ref[:, at] = grad


def same(a, b):
    return jnp.where(a == b, 1.0, 0.0)


def last(v):
    return v[v.shape[0] - 1 :]


def tail_is_long(docs):
    count = jnp.sum(same(docs[:, :1], last(docs)[:, :1]), axis=0, keepdims=True)
    return count > docs.shape[0] // 2


def choose(flag, a, b):
    return jnp.where(jnp.broadcast_to(jnp.where(flag, 1.0, 0.0), a.shape) > 0.5, a, b)


def own_numbers(decay_ref, doc_ref):
    heads, tokens = decay_ref.shape
    docs = jnp.broadcast_to(doc_ref[...].astype(F32) + 1.0, (tokens, tokens)).T
    return cumulative(decay_ref[...]), docs[:, :heads]


def far_kernel(
    head_width,
    decay_ref,
    doc_ref,
    read_ref,
    write_ref,
    read2_ref,
    aux1_ref,
    write2_ref,
    aux2_ref,
    x_ref,
    cot_ref,
    ahead_ref,
    behind_ref,
):
    tokens, cols = x_ref.shape
    heads = decay_ref.shape[0]
    half = tokens // 2
    lam, docs = own_numbers(decay_ref, doc_ref)
    lam1, doc1 = aux_parts(aux1_ref[...], heads)
    _, doc2 = aux_parts(aux2_ref[...], heads)
    gain = jnp.exp(last(lam1)) * same(last(doc1), last(doc2))
    exit_w = thirds(jnp.exp(last(lam) - lam) * same(docs, last(docs)))
    entry = thirds(jnp.exp(lam) * same(docs, last(doc1)) * gain)
    ahead_score = dot(read2_ref[:half], write_ref[...], NT).astype(BF16)
    behind_score = dot(write2_ref[half:], read_ref[...], NT).astype(BF16)
    ahead_sums = tail_is_long(docs)
    behind_rows = tail_is_long(doc2)
    step = min(cols // 2, 512)
    for low in range(0, cols, step):
        at = slice(low, low + step)
        to_cols = spread(heads, head_width, low, step)
        x = (x_ref[:, at].astype(F32) * dot(exit_w, to_cols)).astype(BF16)
        sums = dot(ahead_score, x)
        ahead_ref[:, at] = choose(ahead_sums, sums, x[half:].astype(F32)).astype(BF16)
        cot = (cot_ref[:, at].astype(F32) * dot(entry, to_cols)).astype(BF16)
        sums = dot(behind_score, cot)
        row = low // (cols // 2) * half
        col = low % (cols // 2)
        behind_ref[row : row + half, col : col + step] = choose(
            behind_rows, cot[:half].astype(F32), sums
        ).astype(BF16)


def carried_kernel(
    head_width,
    decay_ref,
    doc_ref,
    read_ref,
    write1_ref,
    aux1_ref,
    write2_ref,
    aux2_ref,
    odd_ref,
    first_ref,
    then_ref,
    x2_ref,
    mixed_ref,
    out_ref,
):
    tokens, cols = first_ref.shape
    odd = odd_ref[0, 0] == 1
    heads = decay_ref.shape[0]
    half = tokens // 2
    lam, docs = own_numbers(decay_ref, doc_ref)
    lam1, doc1 = aux_parts(aux1_ref[...], heads)
    _, doc2 = aux_parts(aux2_ref[...], heads)
    entry = thirds(jnp.exp(lam) * same(docs, last(doc1)))
    gain = jnp.exp(last(lam1)) * same(last(doc1), last(doc2))
    gain = thirds(jnp.broadcast_to(gain, (16, heads)))
    exit1 = thirds(jnp.exp(last(lam1) - lam1) * same(doc1, last(doc1)))
    score1 = dot(read_ref[...], write1_ref[...], NT).astype(BF16)
    take = jnp.where(iota((tokens, half), 0) == iota((tokens, half), 1), 1.0, 0.0)
    score2 = dot(read_ref[...], write2_ref[half:], NT)
    score2 = choose(tail_is_long(doc2), take, score2).astype(BF16)
    step = min(cols, 512)
    for low in range(0, cols, step):
        at = slice(low, low + step)
        to_cols = spread(heads, head_width, low, step)
        x1 = jnp.where(odd, first_ref[:, at], then_ref[:, at])
        x1 = (x1.astype(F32) * dot(exit1, to_cols)).astype(BF16)
        carried = dot(score2, x2_ref[:, at]) * dot(gain, to_cols)[:1]
        carried = (carried + dot(score1, x1)) * dot(entry, to_cols)
        out_ref[:, at] = (mixed_ref[:, at] + carried).astype(BF16)


def returned_kernel(
    head_width,
    decay_ref,
    doc_ref,
    write_ref,
    read2_ref,
    r1_ref,
    r2_ref,
    own_ref,
    odd_ref,
    first_ref,
    then_ref,
    grad_ref,
    out_ref,
    grad_key_ref,
    grad_value_ref,
):
    tokens, cols = first_ref.shape
    odd = odd_ref[0, 0] == 1
    heads = decay_ref.shape[0]
    state = write_ref.shape[1]
    half = tokens // 2
    width = HEAD_CHANNELS
    kv2 = own_ref.shape[1]
    total = own_ref[...] + r1_ref[:, :kv2].astype(F32) + r2_ref[:, :kv2].astype(F32)
    for g in range(kv2 // (2 * width)):
        at = slice(g * width, (g + 1) * width)
        low = 2 * g * width
        grad_key_ref[:, at] = total[:, low : low + width].astype(BF16)
        grad_value_ref[:, at] = total[:, low + width : low + 2 * width].astype(BF16)
    lam, docs = own_numbers(decay_ref, doc_ref)
    lam1, doc1 = aux_parts(r1_ref[:, kv2 + state :], heads)
    exit_w = thirds(jnp.exp(last(lam) - lam) * same(docs, last(docs)))
    entry1 = thirds(jnp.exp(lam1) * same(doc1, last(docs)))
    score1 = dot(write_ref[...], r1_ref[:, kv2 : kv2 + state], NT).astype(BF16)
    take = jnp.where(iota((tokens, half), 0) == iota((tokens, half), 1) + half, 1.0, 0.0)
    score2 = dot(write_ref[...], read2_ref[:half], NT)
    score2 = choose(tail_is_long(docs), score2, take).astype(BF16)
    step = min(cols // 2, 512)
    for low in range(0, cols, step):
        at = slice(low, low + step)
        to_cols = spread(heads, head_width, low, step)
        c1 = jnp.where(odd, then_ref[:, at], first_ref[:, at])
        c1 = (c1.astype(F32) * dot(entry1, to_cols)).astype(BF16)
        row = low // (cols // 2) * half
        col = kv2 + low % (cols // 2)
        far = r2_ref[row : row + half, col : col + step]
        returned = (dot(score1, c1) + dot(score2, far)) * dot(exit_w, to_cols)
        out_ref[:, at] = (grad_ref[:, at] + returned).astype(BF16)


def whole(shape):
    return pl.BlockSpec(shape, lambda i: (0, 0))


def columns(rows, cols):
    return pl.BlockSpec((rows, cols), lambda i: (0, i))


def part(rows, width, low):
    return pl.BlockSpec((rows, width), lambda i: (0, low // width))


def shards(
    query_head_matrix,
    key_head_matrix,
    value_head_matrix,
    ssm_input,
    log_decay,
    state_write,
    state_read,
    document_ids,
    attention_output_gradient,
    cot_mixer,
):
    tokens, kv = key_head_matrix.shape
    kv_local = kv // HEAD_CHANNELS
    heads = log_decay.shape[1]
    state = state_write.shape[1]
    cols = ssm_input.shape[1]
    head_width = cols // heads
    group_cols = query_head_matrix.shape[1] // kv_local
    doc_row = document_ids.reshape(1, tokens)
    decay_t = log_decay.T
    aux = 4 * heads
    m_cols = 2 * kv + state + aux
    step_cols = min(512, cols)
    steps = cols // step_cols
    shape = jax.ShapeDtypeStruct
    params = pltpu.CompilerParams(vmem_limit_bytes=VMEM_LIMIT)

    odd = lax.axis_index("ctx") % 2
    first_sent = jnp.where(odd == 0, ssm_input, cot_mixer)
    then_sent = jnp.where(odd == 0, cot_mixer, ssm_input)
    odd = odd.reshape(1, 1)
    first = exchanged(first_sent, "ctx", 0)
    m0, n0 = pl.pallas_call(
        pack_kernel,
        out_shape=(shape((tokens, m_cols), BF16),) * 2,
        compiler_params=pltpu.CompilerParams(vmem_limit_bytes=PACK_LIMIT),
        name="pack",
    )(key_head_matrix, value_head_matrix, state_write, state_read, decay_t, doc_row)
    m1 = passed_along(m0, "ctx", 1)
    m2 = passed_along(m0, "ctx", 2)
    read2 = passed_along(n0, "ctx", -2)
    then = exchanged(then_sent, "ctx", 1)
    decay_local, m1, m2, read2 = lax.optimization_barrier((decay_t, m1, m2, read2))
    mixed, grad = pl.pallas_call(
        functools.partial(local_kernel, head_width),
        grid=(steps,),
        in_specs=[
            whole((1, tokens)),
            whole((tokens, state)),
            whole((tokens, state)),
            pl.BlockSpec((heads // steps, tokens), lambda i: (i, 0)),
            columns(tokens, step_cols),
            columns(tokens, step_cols),
        ],
        out_specs=[columns(tokens, step_cols)] * 2,
        out_shape=(shape(ssm_input.shape, F32),) * 2,
        compiler_params=params,
        name="local_mixer",
    )(doc_row, state_write, state_read, decay_local, ssm_input, cot_mixer)

    write_at = 2 * kv
    ahead, behind = pl.pallas_call(
        functools.partial(far_kernel, head_width),
        grid=(1,),
        in_specs=[
            whole((heads, tokens)),
            whole((1, tokens)),
            whole((tokens, state)),
            whole((tokens, state)),
            part(tokens, state, 0),
            part(tokens, aux, write_at + state),
            part(tokens, state, write_at),
            part(tokens, aux, write_at + state),
            whole((tokens, cols)),
            whole((tokens, cols)),
        ],
        out_specs=[whole((tokens // 2, cols)), whole((tokens, cols // 2))],
        out_shape=(
            shape((tokens // 2, cols), BF16),
            shape((tokens, cols // 2), BF16),
        ),
        compiler_params=params,
        name="far",
    )(decay_t, doc_row, state_read, state_write, read2, m1, m2, m2, ssm_input, cot_mixer)
    x2 = passed_along(ahead, "ctx", 2)
    attention_out, own, back1, back2 = pl.pallas_call(
        functools.partial(attn_kernel, kv, 2 * kv + state + 3 * heads),
        grid=(kv_local,),
        in_specs=[whole((1, tokens)), whole((tokens, state))]
        + [whole((tokens, m_cols))] * 3
        + [columns(tokens, group_cols)] * 2
        + [whole((tokens, cols // 2))],
        out_specs=[
            columns(tokens, group_cols),
            whole((tokens, 2 * kv)),
            whole((tokens, m_cols)),
            whole((tokens, 2 * kv + cols // 2)),
        ],
        out_shape=(
            shape(query_head_matrix.shape, BF16),
            shape((tokens, 2 * kv), F32),
            shape((tokens, m_cols), BF16),
            shape((tokens, 2 * kv + cols // 2), BF16),
        ),
        compiler_params=params,
        name="attention",
    )(doc_row, state_read, m0, m1, m2, query_head_matrix, attention_output_gradient, behind)
    r1 = passed_along(back1, "ctx", -1)
    r2 = passed_along(back2, "ctx", -2)


    mixer_out = pl.pallas_call(
        functools.partial(carried_kernel, head_width),
        grid=(1,),
        in_specs=[
            whole((heads, tokens)),
            whole((1, tokens)),
            whole((tokens, state)),
            part(tokens, state, write_at),
            part(tokens, aux, write_at + state),
            part(tokens, state, write_at),
            part(tokens, aux, write_at + state),
            pl.BlockSpec(memory_space=pltpu.SMEM),
            whole((tokens, cols)),
            whole((tokens, cols)),
            whole((tokens // 2, cols)),
            whole((tokens, cols)),
        ],
        out_specs=whole((tokens, cols)),
        out_shape=shape(ssm_input.shape, BF16),
        compiler_params=params,
        name="carried",
    )(decay_t, doc_row, state_read, m1, m1, m2, m2, odd, first, then, x2, mixed)

    own, mixer_out = lax.optimization_barrier((own, mixer_out))
    grad_input, grad_key, grad_value = pl.pallas_call(
        functools.partial(returned_kernel, head_width),
        grid=(1,),
        in_specs=[
            whole((heads, tokens)),
            whole((1, tokens)),
            whole((tokens, state)),
            part(tokens, state, 0),
            whole((tokens, m_cols)),
            whole((tokens, 2 * kv + cols // 2)),
            whole((tokens, 2 * kv)),
            pl.BlockSpec(memory_space=pltpu.SMEM),
            whole((tokens, cols)),
            whole((tokens, cols)),
            whole((tokens, cols)),
        ],
        out_specs=[whole((tokens, cols))] + [whole((tokens, kv))] * 2,
        out_shape=(
            shape(cot_mixer.shape, BF16),
            shape(key_head_matrix.shape, BF16),
            shape(value_head_matrix.shape, BF16),
        ),
        compiler_params=params,
        name="returned",
    )(decay_t, doc_row, state_write, read2, r1, r2, own, odd, first, then, grad)
    return (attention_out, mixer_out, grad_key, grad_value, grad_input)


def solution(mesh):
    return jax.shard_map(
        shards,
        mesh=mesh,
        in_specs=(
            P("ctx", "tp"),
            P("ctx", "tp"),
            P("ctx", "tp"),
            P("ctx", "tp"),
            P("ctx", "tp"),
            P("ctx", None),
            P("ctx", None),
            P("ctx"),
            P("ctx", "tp"),
            P("ctx", "tp"),
        ),
        out_specs=(P("ctx", "tp"), P("ctx", "tp"), P("ctx", "tp"), P("ctx", "tp"), P("ctx", "tp")),
        check_vma=False,
    )
```

```python
import functools
import math

import jax
import jax.numpy as jnp
from jax import lax
from jax.experimental import pallas as pl
from jax.experimental.pallas import tpu as pltpu
from jax.sharding import PartitionSpec as P

HEAD_CHANNELS = 128
BF16 = jnp.bfloat16
F32 = jnp.float32
VMEM_LIMIT = 20 * 1024 * 1024
PACK_LIMIT = 60 * 1024 * 1024
NT = (((1,), (1,)), ((), ()))
TN = (((0,), (0,)), ((), ()))


def passed_along(block, axis, distance):
    devices = range(lax.axis_size(axis))
    route = [(i - distance, i) for i in devices if i - distance in devices]
    return lax.ppermute(block, axis, route)


def exchanged(block, axis, first):
    count = lax.axis_size(axis)
    route = []
    for i in range(first, count - 1, 2):
        route += [(i, i + 1), (i + 1, i)]
    return lax.ppermute(block, axis, route)


def dot(a, b, dims=(((1,), (0,)), ((), ()))):
    return lax.dot_general(a, b, dims, preferred_element_type=F32)


def iota(shape, dim):
    return lax.broadcasted_iota(jnp.int32, shape, dim)


def split3(v):
    hi = v.astype(BF16)
    rest = v - hi.astype(F32)
    mid = rest.astype(BF16)
    lo = (rest - mid.astype(F32)).astype(BF16)
    return hi, mid, lo


def cumulative(decay_t):
    tokens = decay_t.shape[1]
    tri = iota((tokens, tokens), 0) >= iota((tokens, tokens), 1)
    tri = jnp.where(tri, 1.0, 0.0).astype(BF16)
    return sum(dot(tri, part, NT) for part in split3(decay_t))


def thirds(v):
    return jnp.concatenate([part.astype(F32) for part in split3(v)], axis=1).astype(BF16)


def spread(heads, head_width, low, cols):
    offset = iota((heads, cols), 1) + low - iota((heads, cols), 0) * head_width
    match = jnp.where((offset >= 0) & (offset < head_width), 1.0, 0.0)
    return jnp.concatenate([match] * 3, axis=0).astype(BF16)


def aux_parts(aux, heads):
    wide = aux.astype(F32)
    lam = wide[:, :heads] + wide[:, heads : 2 * heads] + wide[:, 2 * heads : 3 * heads]
    return lam, wide[:, 3 * heads : 4 * heads]


def pack_kernel(key_ref, value_ref, write_ref, decay_ref, doc_ref, m_ref):
    tokens, kv = key_ref.shape
    heads = decay_ref.shape[0]
    state = write_ref.shape[1]
    lam = cumulative(decay_ref[...])
    docs = jnp.broadcast_to(doc_ref[...].astype(F32) + 1.0, (tokens, tokens)).T[:, :heads]
    aux = jnp.concatenate([p.astype(F32) for p in split3(lam)] + [docs], axis=1).astype(BF16)
    m_ref[:, :kv] = key_ref[...]
    m_ref[:, kv : 2 * kv] = value_ref[...]
    m_ref[:, 2 * kv : 2 * kv + state] = write_ref[...]
    m_ref[:, 2 * kv + state :] = aux


def attn_kernel(
    kv,
    docs_at,
    doc_ref,
    read_ref,
    m0,
    m1,
    m2,
    q_ref,
    cot_ref,
    far_ref,
    entry_ref,
    out_ref,
    own_ref,
    back1_ref,
    back2_ref,
):
    tokens = m0.shape[0]
    group = q_ref.shape[1] // HEAD_CHANNELS
    inv_root = 1.0 / math.sqrt(HEAD_CHANNELS)
    width = HEAD_CHANNELS
    tiles = (m2, m1, m0)
    key_cols = pl.ds(pl.multiple_of(pl.program_id(0) * width, width), width)
    value_cols = pl.ds(pl.multiple_of(kv + pl.program_id(0) * width, width), width)
    keys = jnp.concatenate([tile[:, key_cols] for tile in tiles], axis=0)
    values = jnp.concatenate([tile[:, value_cols] for tile in tiles], axis=0)
    span = keys.shape[0]
    doc_s = jnp.concatenate(
        [tile[:, docs_at : docs_at + 1].astype(F32) for tile in tiles], axis=0
    )
    doc_t = doc_ref[...].astype(F32) + 1.0
    inside = (doc_s == doc_t) & (
        iota((span, tokens), 0) - (span - tokens) <= iota((span, tokens), 1)
    )
    inside = jnp.where(inside, 1.0, 0.0)
    inside = jnp.concatenate([inside] * group, axis=1) > 0.5
    query = jnp.concatenate(
        [q_ref[:, i * width : (i + 1) * width] for i in range(group)], axis=0
    )
    cot = jnp.concatenate(
        [cot_ref[:, i * width : (i + 1) * width] for i in range(group)], axis=0
    )
    score = jnp.where(inside, dot(keys, query, NT) * inv_root, -1e30)
    raised = jnp.exp(score - jnp.max(score, axis=0, keepdims=True))
    prob = (raised * (1.0 / jnp.sum(raised, axis=0, keepdims=True))).astype(BF16)
    out = dot(values, prob, TN).T
    for i in range(group):
        out_ref[:, i * width : (i + 1) * width] = out[i * tokens : (i + 1) * tokens].astype(BF16)
    prob_grad = dot(values, cot, NT)
    prob32 = prob.astype(F32)
    inner = jnp.sum(prob32 * prob_grad, axis=0, keepdims=True)
    score_grad = (prob32 * (prob_grad - inner) * inv_root).astype(BF16)
    key_grad = dot(score_grad, query)
    value_grad = dot(prob, cot)
    low = pl.multiple_of(pl.program_id(0) * 2 * width, 2 * width)
    key_at = pl.ds(low, width)
    value_at = pl.ds(pl.multiple_of(low + width, width), width)
    back2_ref[:, key_at] = key_grad[:tokens].astype(BF16)
    back2_ref[:, value_at] = value_grad[:tokens].astype(BF16)
    back1_ref[:, key_at] = key_grad[tokens : 2 * tokens].astype(BF16)
    back1_ref[:, value_at] = value_grad[tokens : 2 * tokens].astype(BF16)
    own_ref[:, key_at] = key_grad[2 * tokens :]
    own_ref[:, value_at] = value_grad[2 * tokens :]

    @pl.when(pl.program_id(0) == 0)
    def _():
        state = read_ref.shape[1]
        back1_ref[:, 2 * kv : 2 * kv + state] = read_ref[...]
        back1_ref[:, 2 * kv + state :] = entry_ref[...]
        back2_ref[:, 2 * kv :] = far_ref[...]


def local_kernel(
    heads,
    head_width,
    doc_ref,
    write_ref,
    read_ref,
    decay_ref,
    aux1_ref,
    aux2_ref,
    x_ref,
    cot_ref,
    mixed_ref,
    grad_ref,
    entry_ref,
    exit_ref,
    exit1_ref,
    gain_ref,
):
    tokens, cols = x_ref.shape
    step_heads = cols // head_width
    lam = cumulative(decay_ref[...])
    upper = iota((tokens, tokens), 0) <= iota((tokens, tokens), 1)
    upper = jnp.where(upper, 1.0, 0.0).astype(BF16)
    lam_t = sum(dot(part, upper) for part in split3(decay_ref[...]))
    doc_row = doc_ref[...].astype(F32)
    doc_col = jnp.broadcast_to(doc_row, (tokens, tokens)).T
    inside = (iota((tokens, tokens), 0) >= iota((tokens, tokens), 1)) & (doc_col == doc_row)
    score = dot(read_ref[...], write_ref[...], NT)
    lam1, doc1 = aux_parts(aux1_ref[...], heads)
    _, doc2 = aux_parts(aux2_ref[...], heads)
    docs = doc_col[:, :step_heads] + 1.0
    entry = jnp.exp(lam) * same(docs, last(doc1)[:, :1])
    exit_w = jnp.exp(last(lam) - lam) * same(docs, last(docs))
    to_cols = spread(step_heads, head_width, 0, cols)
    entry_ref[...] = dot(thirds(entry), to_cols)
    exit_ref[...] = dot(thirds(exit_w), to_cols)
    exit1 = jnp.exp(last(lam1) - lam1) * same(doc1, last(doc1))
    gain = jnp.exp(last(lam1)) * same(last(doc1), last(doc2))
    gain = thirds(jnp.broadcast_to(gain, (16, heads)))
    to_cols = spread(heads, head_width, pl.program_id(0) * cols, cols)
    exit1_ref[...] = dot(thirds(exit1), to_cols)
    gain_ref[...] = dot(gain, to_cols)[:8]
    per = HEAD_CHANNELS // head_width
    lane_head = iota((tokens, HEAD_CHANNELS), 1) // head_width
    for pair in range(step_heads // per):
        at = slice(pair * HEAD_CHANNELS, (pair + 1) * HEAD_CHANNELS)
        x = x_ref[:, at]
        cot = cot_ref[:, at]
        mixed = grad = None
        for j in range(per):
            head = pair * per + j
            gap = lam[:, head : head + 1] - lam_t[head : head + 1, :]
            weights = (jnp.exp(jnp.where(inside, gap, -jnp.inf)) * score).astype(BF16)
            mixed_j = dot(weights, x)
            grad_j = dot(weights, cot, TN)
            mixed = mixed_j if j == 0 else jnp.where(lane_head == j, mixed_j, mixed)
            grad = grad_j if j == 0 else jnp.where(lane_head == j, grad_j, grad)
        mixed_ref[:, at] = mixed
        grad_ref[:, at] = grad


def same(a, b):
    return jnp.where(a == b, 1.0, 0.0)


def last(v):
    return v[v.shape[0] - 1 :]


def tail_is_long(docs):
    count = jnp.sum(same(docs[:, :1], last(docs)[:, :1]), axis=0, keepdims=True)
    return count > docs.shape[0] // 2


def choose(flag, a, b):
    return jnp.where(jnp.broadcast_to(jnp.where(flag, 1.0, 0.0), a.shape) > 0.5, a, b)


def own_numbers(decay_ref, doc_ref):
    heads, tokens = decay_ref.shape
    docs = jnp.broadcast_to(doc_ref[...].astype(F32) + 1.0, (tokens, tokens)).T
    return cumulative(decay_ref[...]), docs[:, :heads]


def far_kernel(
    head_width,
    decay_ref,
    doc_ref,
    read_ref,
    write_ref,
    read2_ref,
    aux1_ref,
    write2_ref,
    aux2_ref,
    x_ref,
    cot_ref,
    ahead_ref,
    behind_ref,
    entry_ref,
    take_ref,
):
    tokens, cols = x_ref.shape
    heads = decay_ref.shape[0]
    half = tokens // 2
    lam, docs = own_numbers(decay_ref, doc_ref)
    lam1, doc1 = aux_parts(aux1_ref[...], heads)
    _, doc2 = aux_parts(aux2_ref[...], heads)
    gain = jnp.exp(last(lam1)) * same(last(doc1), last(doc2))
    exit_w = thirds(jnp.exp(last(lam) - lam) * same(docs, last(docs)))
    entry = jnp.exp(lam) * same(docs, last(doc1))
    parts = [p.astype(F32) for p in split3(entry)] + [jnp.zeros_like(entry)]
    entry_ref[...] = jnp.concatenate(parts, axis=1).astype(BF16)
    entry = thirds(entry * gain)
    take = jnp.where(iota((tokens, half), 0) == iota((tokens, half), 1) + half, 1.0, 0.0)
    sums = dot(write_ref[...], read2_ref[:half], NT)
    take_ref[...] = choose(tail_is_long(docs), sums, take).astype(BF16)
    ahead_score = dot(read2_ref[:half], write_ref[...], NT).astype(BF16)
    behind_score = dot(write2_ref[half:], read_ref[...], NT).astype(BF16)
    ahead_sums = tail_is_long(docs)
    behind_rows = tail_is_long(doc2)
    step = min(cols // 2, 512)
    for low in range(0, cols, step):
        at = slice(low, low + step)
        to_cols = spread(heads, head_width, low, step)
        x = (x_ref[:, at].astype(F32) * dot(exit_w, to_cols)).astype(BF16)
        sums = dot(ahead_score, x)
        ahead_ref[:, at] = choose(ahead_sums, sums, x[half:].astype(F32)).astype(BF16)
        cot = (cot_ref[:, at].astype(F32) * dot(entry, to_cols)).astype(BF16)
        sums = dot(behind_score, cot)
        row = low // (cols // 2) * half
        col = low % (cols // 2)
        behind_ref[row : row + half, col : col + step] = choose(
            behind_rows, cot[:half].astype(F32), sums
        ).astype(BF16)


def in_steps(cols, step, out_ref, held_ref, sems, columns_of):
    copies = []
    for place, low in enumerate(range(0, cols, step)):
        at = slice(low, low + step)
        held_ref[:, at] = columns_of(low, at)
        copies.append(
            pltpu.make_async_copy(held_ref.at[:, at], out_ref.at[:, at], sems.at[place])
        )
        copies[-1].start()
    for copy in copies:
        copy.wait()


def carried_kernel(
    step,
    read_ref,
    write1_ref,
    write2_ref,
    aux2_ref,
    odd_ref,
    first_ref,
    then_ref,
    x2_ref,
    mixed_ref,
    entry_ref,
    exit1_ref,
    gain_ref,
    out_ref,
    held_ref,
    sems,
):
    tokens, cols = first_ref.shape
    half = tokens // 2
    odd = odd_ref[0, 0] == 1
    _, doc2 = aux_parts(aux2_ref[...], aux2_ref.shape[1] // 4)
    score1 = dot(read_ref[...], write1_ref[...], NT).astype(BF16)
    take = jnp.where(iota((tokens, half), 0) == iota((tokens, half), 1), 1.0, 0.0)
    score2 = dot(read_ref[...], write2_ref[half:], NT)
    score2 = choose(tail_is_long(doc2), take, score2).astype(BF16)

    def columns_of(low, at):
        x1 = jnp.where(odd, first_ref[:, at], then_ref[:, at])
        x1 = (x1.astype(F32) * exit1_ref[:, at]).astype(BF16)
        carried = dot(score2, x2_ref[:, at]) * gain_ref[:1, at] + dot(score1, x1)
        return (mixed_ref[:, at] + carried * entry_ref[:, at]).astype(BF16)

    in_steps(cols, step, out_ref, held_ref, sems, columns_of)


def returned_kernel(
    heads,
    head_width,
    step,
    write_ref,
    take_ref,
    r1_ref,
    r2_ref,
    own_ref,
    odd_ref,
    first_ref,
    then_ref,
    grad_ref,
    exit_ref,
    out_ref,
    grad_key_ref,
    grad_value_ref,
):
    cols = first_ref.shape[1]
    state = write_ref.shape[1]
    half = take_ref.shape[1]
    odd = odd_ref[0, 0] == 1
    width = HEAD_CHANNELS
    kv2 = own_ref.shape[1]
    score1 = dot(write_ref[...], r1_ref[:, kv2 : kv2 + state], NT).astype(BF16)
    entry1 = r1_ref[:, kv2 + state : kv2 + state + 3 * heads]
    total = own_ref[...] + r1_ref[:, :kv2].astype(F32) + r2_ref[:, :kv2].astype(F32)
    for g in range(kv2 // (2 * width)):
        at = slice(g * width, (g + 1) * width)
        low = 2 * g * width
        grad_key_ref[:, at] = total[:, low : low + width].astype(BF16)
        grad_value_ref[:, at] = total[:, low + width : low + 2 * width].astype(BF16)

    def columns_of(low, at):
        c1 = jnp.where(odd, then_ref[:, at], first_ref[:, at])
        entry = dot(entry1, spread(heads, head_width, low, step))
        c1 = (c1.astype(F32) * entry).astype(BF16)
        row = low // (cols // 2) * half
        col = kv2 + low % (cols // 2)
        far = r2_ref[row : row + half, col : col + step]
        returned = dot(score1, c1) + dot(take_ref[...], far)
        return (grad_ref[:, at] + returned * exit_ref[:, at]).astype(BF16)

    for low in range(0, cols, step):
        at = slice(low, low + step)
        out_ref[:, at] = columns_of(low, at)

def whole(shape):
    return pl.BlockSpec(shape, lambda i: (0, 0))


def columns(rows, cols):
    return pl.BlockSpec((rows, cols), lambda i: (0, i))


def part(rows, width, low):
    return pl.BlockSpec((rows, width), lambda i: (0, low // width))


def shards(
    query_head_matrix,
    key_head_matrix,
    value_head_matrix,
    ssm_input,
    log_decay,
    state_write,
    state_read,
    document_ids,
    attention_output_gradient,
    cot_mixer,
):
    tokens, kv = key_head_matrix.shape
    kv_local = kv // HEAD_CHANNELS
    heads = log_decay.shape[1]
    state = state_write.shape[1]
    cols = ssm_input.shape[1]
    head_width = cols // heads
    group_cols = query_head_matrix.shape[1] // kv_local
    doc_row = document_ids.reshape(1, tokens)
    decay_t = log_decay.T
    aux = 4 * heads
    m_cols = 2 * kv + state + aux
    step_cols = min(512, cols)
    steps = cols // step_cols
    shape = jax.ShapeDtypeStruct
    params = pltpu.CompilerParams(vmem_limit_bytes=VMEM_LIMIT)

    odd = lax.axis_index("ctx") % 2
    read2 = passed_along(state_read, "ctx", -2)
    m0 = pl.pallas_call(
        pack_kernel,
        out_shape=shape((tokens, m_cols), BF16),
        compiler_params=pltpu.CompilerParams(vmem_limit_bytes=PACK_LIMIT),
        name="pack",
    )(key_head_matrix, value_head_matrix, state_write, decay_t, doc_row)
    m1 = passed_along(m0, "ctx", 1)
    m2 = passed_along(m0, "ctx", 2)
    x0, cot0, read2 = lax.optimization_barrier((ssm_input, cot_mixer, read2))
    first_sent = jnp.where(odd == 0, x0, cot0)
    then_sent = jnp.where(odd == 0, cot0, x0)
    odd = odd.reshape(1, 1)
    first = exchanged(first_sent, "ctx", 0)
    then = exchanged(then_sent, "ctx", 1)
    decay_local, m1, m2, read2 = lax.optimization_barrier((decay_t, m1, m2, read2))
    write_at = 2 * kv
    mixed, grad, entry_w, exit_w, exit1_w, gain_w = pl.pallas_call(
        functools.partial(local_kernel, heads, head_width),
        grid=(steps,),
        in_specs=[
            whole((1, tokens)),
            whole((tokens, state)),
            whole((tokens, state)),
            pl.BlockSpec((heads // steps, tokens), lambda i: (i, 0)),
            part(tokens, aux, write_at + state),
            part(tokens, aux, write_at + state),
            columns(tokens, step_cols),
            columns(tokens, step_cols),
        ],
        out_specs=[columns(tokens, step_cols)] * 5 + [columns(8, step_cols)],
        out_shape=(shape(ssm_input.shape, F32),) * 5 + (shape((8, cols), F32),),
        compiler_params=params,
        name="local_mixer",
    )(doc_row, state_write, state_read, decay_local, m1, m2, ssm_input, cot_mixer)

    ahead, behind, entry_parts, take2 = pl.pallas_call(
        functools.partial(far_kernel, head_width),
        grid=(1,),
        in_specs=[
            whole((heads, tokens)),
            whole((1, tokens)),
            whole((tokens, state)),
            whole((tokens, state)),
            whole((tokens, state)),
            part(tokens, aux, write_at + state),
            part(tokens, state, write_at),
            part(tokens, aux, write_at + state),
            whole((tokens, cols)),
            whole((tokens, cols)),
        ],
        out_specs=[
            whole((tokens // 2, cols)),
            whole((tokens, cols // 2)),
            whole((tokens, aux)),
            whole((tokens, tokens // 2)),
        ],
        out_shape=(
            shape((tokens // 2, cols), BF16),
            shape((tokens, cols // 2), BF16),
            shape((tokens, aux), BF16),
            shape((tokens, tokens // 2), BF16),
        ),
        compiler_params=params,
        name="far",
    )(decay_t, doc_row, state_read, state_write, read2, m1, m2, m2, ssm_input, cot_mixer)
    x2 = passed_along(ahead, "ctx", 2)
    attention_out, own, back1, back2 = pl.pallas_call(
        functools.partial(attn_kernel, kv, 2 * kv + state + 3 * heads),
        grid=(kv_local,),
        in_specs=[whole((1, tokens)), whole((tokens, state))]
        + [whole((tokens, m_cols))] * 3
        + [columns(tokens, group_cols)] * 2
        + [whole((tokens, cols // 2)), whole((tokens, aux))],
        out_specs=[
            columns(tokens, group_cols),
            whole((tokens, 2 * kv)),
            whole((tokens, m_cols)),
            whole((tokens, 2 * kv + cols // 2)),
        ],
        out_shape=(
            shape(query_head_matrix.shape, BF16),
            shape((tokens, 2 * kv), F32),
            shape((tokens, m_cols), BF16),
            shape((tokens, 2 * kv + cols // 2), BF16),
        ),
        compiler_params=params,
        name="attention",
    )(doc_row, state_read, m0, m1, m2, query_head_matrix, attention_output_gradient, behind, entry_parts)
    r1 = passed_along(back1, "ctx", -1)
    r2 = passed_along(back2, "ctx", -2)


    smem = pl.BlockSpec(memory_space=pltpu.SMEM)
    half_step = min(step_cols, cols // 2)
    held = [
        pltpu.VMEM((tokens, cols), BF16),
        pltpu.SemaphoreType.DMA((cols // half_step,)),
    ]
    mixer_out = pl.pallas_call(
        functools.partial(carried_kernel, half_step),
        grid=(1,),
        in_specs=[
            whole((tokens, state)),
            part(tokens, state, write_at),
            part(tokens, state, write_at),
            part(tokens, aux, write_at + state),
            smem,
            whole((tokens, cols)),
            whole((tokens, cols)),
            whole((tokens // 2, cols)),
        ]
        + [whole((tokens, cols))] * 3
        + [whole((8, cols))],
        out_specs=pl.BlockSpec(memory_space=pl.ANY),
        out_shape=shape(ssm_input.shape, BF16),
        scratch_shapes=held,
        compiler_params=params,
        name="carried",
    )(state_read, m1, m2, m2, odd, first, then, x2, mixed, entry_w, exit1_w, gain_w)

    own, mixer_out = lax.optimization_barrier((own, mixer_out))
    grad_input, grad_key, grad_value = pl.pallas_call(
        functools.partial(returned_kernel, heads, head_width, half_step),
        grid=(1,),
        in_specs=[
            whole((tokens, state)),
            whole((tokens, tokens // 2)),
            whole((tokens, m_cols)),
            whole((tokens, 2 * kv + cols // 2)),
            whole((tokens, 2 * kv)),
            smem,
        ]
        + [whole((tokens, cols))] * 4,
        out_specs=[whole((tokens, cols))] + [whole((tokens, kv))] * 2,
        out_shape=(
            shape(cot_mixer.shape, BF16),
            shape(key_head_matrix.shape, BF16),
            shape(value_head_matrix.shape, BF16),
        ),
        compiler_params=params,
        name="returned",
    )(state_write, take2, r1, r2, own, odd, first, then, grad, exit_w)
    return (attention_out, mixer_out, grad_key, grad_value, grad_input)


def solution(mesh):
    return jax.shard_map(
        shards,
        mesh=mesh,
        in_specs=(
            P("ctx", "tp"),
            P("ctx", "tp"),
            P("ctx", "tp"),
            P("ctx", "tp"),
            P("ctx", "tp"),
            P("ctx", None),
            P("ctx", None),
            P("ctx"),
            P("ctx", "tp"),
            P("ctx", "tp"),
        ),
        out_specs=(P("ctx", "tp"), P("ctx", "tp"), P("ctx", "tp"), P("ctx", "tp"), P("ctx", "tp")),
        check_vma=False,
    )
```

```python
import functools
import math

import jax
import jax.numpy as jnp
from jax import lax
from jax.experimental import pallas as pl
from jax.experimental.pallas import tpu as pltpu
from jax.sharding import PartitionSpec as P

HEAD_CHANNELS = 128
BF16 = jnp.bfloat16
F32 = jnp.float32
VMEM_LIMIT = 20 * 1024 * 1024
PACK_LIMIT = 60 * 1024 * 1024
NT = (((1,), (1,)), ((), ()))
TN = (((0,), (0,)), ((), ()))


def passed_along(block, axis, distance):
    devices = range(lax.axis_size(axis))
    route = [(i - distance, i) for i in devices if i - distance in devices]
    return lax.ppermute(block, axis, route)


def exchanged(block, axis, first):
    count = lax.axis_size(axis)
    route = []
    for i in range(first, count - 1, 2):
        route += [(i, i + 1), (i + 1, i)]
    return lax.ppermute(block, axis, route)


def dot(a, b, dims=(((1,), (0,)), ((), ()))):
    return lax.dot_general(a, b, dims, preferred_element_type=F32)


def iota(shape, dim):
    return lax.broadcasted_iota(jnp.int32, shape, dim)


def split3(v):
    hi = v.astype(BF16)
    rest = v - hi.astype(F32)
    mid = rest.astype(BF16)
    lo = (rest - mid.astype(F32)).astype(BF16)
    return hi, mid, lo


def cumulative(decay_t):
    tokens = decay_t.shape[1]
    tri = iota((tokens, tokens), 0) >= iota((tokens, tokens), 1)
    tri = jnp.where(tri, 1.0, 0.0).astype(BF16)
    return sum(dot(tri, part, NT) for part in split3(decay_t))


def thirds(v):
    return jnp.concatenate([part.astype(F32) for part in split3(v)], axis=1).astype(BF16)


def spread(heads, head_width, low, cols):
    offset = iota((heads, cols), 1) + low - iota((heads, cols), 0) * head_width
    match = jnp.where((offset >= 0) & (offset < head_width), 1.0, 0.0)
    return jnp.concatenate([match] * 3, axis=0).astype(BF16)


def aux_parts(aux, heads):
    wide = aux.astype(F32)
    lam = wide[:, :heads] + wide[:, heads : 2 * heads] + wide[:, 2 * heads : 3 * heads]
    return lam, wide[:, 3 * heads : 4 * heads]


def pack_kernel(key_ref, value_ref, write_ref, decay_ref, doc_ref, m_ref):
    tokens, kv = key_ref.shape
    heads = decay_ref.shape[0]
    state = write_ref.shape[1]
    lam = cumulative(decay_ref[...])
    docs = jnp.broadcast_to(doc_ref[...].astype(F32) + 1.0, (tokens, tokens)).T[:, :heads]
    aux = jnp.concatenate([p.astype(F32) for p in split3(lam)] + [docs], axis=1).astype(BF16)
    m_ref[:, :kv] = key_ref[...]
    m_ref[:, kv : 2 * kv] = value_ref[...]
    m_ref[:, 2 * kv : 2 * kv + state] = write_ref[...]
    m_ref[:, 2 * kv + state :] = aux


def attn_kernel(
    kv,
    docs_at,
    doc_ref,
    read_ref,
    m0,
    m1,
    m2,
    q_ref,
    cot_ref,
    far_ref,
    entry_ref,
    out_ref,
    own_ref,
    back1_ref,
    back2_ref,
):
    tokens = m0.shape[0]
    group = q_ref.shape[1] // HEAD_CHANNELS
    inv_root = 1.0 / math.sqrt(HEAD_CHANNELS)
    width = HEAD_CHANNELS
    tiles = (m2, m1, m0)
    key_cols = pl.ds(pl.multiple_of(pl.program_id(0) * width, width), width)
    value_cols = pl.ds(pl.multiple_of(kv + pl.program_id(0) * width, width), width)
    keys = jnp.concatenate([tile[:, key_cols] for tile in tiles], axis=0)
    values = jnp.concatenate([tile[:, value_cols] for tile in tiles], axis=0)
    span = keys.shape[0]
    doc_s = jnp.concatenate(
        [tile[:, docs_at : docs_at + 1].astype(F32) for tile in tiles], axis=0
    )
    doc_t = doc_ref[...].astype(F32) + 1.0
    inside = (doc_s == doc_t) & (
        iota((span, tokens), 0) - (span - tokens) <= iota((span, tokens), 1)
    )
    inside = jnp.where(inside, 1.0, 0.0)
    inside = jnp.concatenate([inside] * group, axis=1) > 0.5
    query = jnp.concatenate(
        [q_ref[:, i * width : (i + 1) * width] for i in range(group)], axis=0
    )
    cot = jnp.concatenate(
        [cot_ref[:, i * width : (i + 1) * width] for i in range(group)], axis=0
    )
    score = jnp.where(inside, dot(keys, query, NT) * inv_root, -1e30)
    raised = jnp.exp(score - jnp.max(score, axis=0, keepdims=True))
    prob = (raised * (1.0 / jnp.sum(raised, axis=0, keepdims=True))).astype(BF16)
    out = dot(values, prob, TN).T
    for i in range(group):
        out_ref[:, i * width : (i + 1) * width] = out[i * tokens : (i + 1) * tokens].astype(BF16)
    prob_grad = dot(values, cot, NT)
    prob32 = prob.astype(F32)
    inner = jnp.sum(prob32 * prob_grad, axis=0, keepdims=True)
    score_grad = (prob32 * (prob_grad - inner) * inv_root).astype(BF16)
    key_grad = dot(score_grad, query)
    value_grad = dot(prob, cot)
    low = pl.multiple_of(pl.program_id(0) * 2 * width, 2 * width)
    key_at = pl.ds(low, width)
    value_at = pl.ds(pl.multiple_of(low + width, width), width)
    back2_ref[:, key_at] = key_grad[:tokens].astype(BF16)
    back2_ref[:, value_at] = value_grad[:tokens].astype(BF16)
    back1_ref[:, key_at] = key_grad[tokens : 2 * tokens].astype(BF16)
    back1_ref[:, value_at] = value_grad[tokens : 2 * tokens].astype(BF16)
    own_ref[:, key_at] = key_grad[2 * tokens :]
    own_ref[:, value_at] = value_grad[2 * tokens :]

    @pl.when(pl.program_id(0) == 0)
    def _():
        state = read_ref.shape[1]
        back1_ref[:, 2 * kv : 2 * kv + state] = read_ref[...]
        back1_ref[:, 2 * kv + state :] = entry_ref[...]
        far_cols = far_ref.shape[1]
        back2_ref[:, 2 * kv : 2 * kv + far_cols] = far_ref[...]
        back2_ref[:, 2 * kv + far_cols :] = read_ref[...]


def local_kernel(
    heads,
    head_width,
    doc_ref,
    write_ref,
    read_ref,
    decay_ref,
    aux1_ref,
    aux2_ref,
    x_ref,
    cot_ref,
    mixed_ref,
    grad_ref,
    entry_ref,
    exit_ref,
    exit1_ref,
    exit2_ref,
):
    tokens, cols = x_ref.shape
    step_heads = cols // head_width
    lam = cumulative(decay_ref[...])
    upper = iota((tokens, tokens), 0) <= iota((tokens, tokens), 1)
    upper = jnp.where(upper, 1.0, 0.0).astype(BF16)
    lam_t = sum(dot(part, upper) for part in split3(decay_ref[...]))
    doc_row = doc_ref[...].astype(F32)
    doc_col = jnp.broadcast_to(doc_row, (tokens, tokens)).T
    inside = (iota((tokens, tokens), 0) >= iota((tokens, tokens), 1)) & (doc_col == doc_row)
    score = dot(read_ref[...], write_ref[...], NT)
    lam1, doc1 = aux_parts(aux1_ref[...], heads)
    lam2, doc2 = aux_parts(aux2_ref[...], heads)
    docs = doc_col[:, :step_heads] + 1.0
    entry = jnp.exp(lam) * same(docs, last(doc1)[:, :1])
    exit_w = jnp.exp(last(lam) - lam) * same(docs, last(docs))
    to_cols = spread(step_heads, head_width, 0, cols)
    entry_ref[...] = dot(thirds(entry), to_cols)
    exit_ref[...] = dot(thirds(exit_w), to_cols)
    exit1 = jnp.exp(last(lam1) - lam1) * same(doc1, last(doc1))
    gain = jnp.exp(last(lam1)) * same(last(doc1), last(doc2))
    exit2 = jnp.exp(last(lam2) - lam2) * same(doc2, last(doc2)) * gain
    to_cols = spread(heads, head_width, pl.program_id(0) * cols, cols)
    exit1_ref[...] = dot(thirds(exit1), to_cols)
    exit2_ref[...] = dot(thirds(exit2), to_cols)
    per = HEAD_CHANNELS // head_width
    lane_head = iota((tokens, HEAD_CHANNELS), 1) // head_width
    for pair in range(step_heads // per):
        at = slice(pair * HEAD_CHANNELS, (pair + 1) * HEAD_CHANNELS)
        x = x_ref[:, at]
        cot = cot_ref[:, at]
        mixed = grad = None
        for j in range(per):
            head = pair * per + j
            gap = lam[:, head : head + 1] - lam_t[head : head + 1, :]
            weights = (jnp.exp(jnp.where(inside, gap, -jnp.inf)) * score).astype(BF16)
            mixed_j = dot(weights, x)
            grad_j = dot(weights, cot, TN)
            mixed = mixed_j if j == 0 else jnp.where(lane_head == j, mixed_j, mixed)
            grad = grad_j if j == 0 else jnp.where(lane_head == j, grad_j, grad)
        mixed_ref[:, at] = mixed
        grad_ref[:, at] = grad


def same(a, b):
    return jnp.where(a == b, 1.0, 0.0)


def last(v):
    return v[v.shape[0] - 1 :]


def tail_is_long(docs):
    count = jnp.sum(same(docs[:, :1], last(docs)[:, :1]), axis=0, keepdims=True)
    return count > docs.shape[0] // 2


def choose(flag, a, b):
    return jnp.where(jnp.broadcast_to(jnp.where(flag, 1.0, 0.0), a.shape) > 0.5, a, b)


def own_numbers(decay_ref, doc_ref):
    heads, tokens = decay_ref.shape
    docs = jnp.broadcast_to(doc_ref[...].astype(F32) + 1.0, (tokens, tokens)).T
    return cumulative(decay_ref[...]), docs[:, :heads]


def far_kernel(
    head_width,
    decay_ref,
    doc_ref,
    read_ref,
    aux1_ref,
    write2_ref,
    aux2_ref,
    cot_ref,
    behind_ref,
    entry_ref,
    long_ref,
):
    tokens, cols = cot_ref.shape
    heads = decay_ref.shape[0]
    half = tokens // 2
    lam, docs = own_numbers(decay_ref, doc_ref)
    lam1, doc1 = aux_parts(aux1_ref[...], heads)
    _, doc2 = aux_parts(aux2_ref[...], heads)
    gain = jnp.exp(last(lam1)) * same(last(doc1), last(doc2))
    entry = jnp.exp(lam) * same(docs, last(doc1))
    parts = [p.astype(F32) for p in split3(entry)] + [jnp.zeros_like(entry)]
    entry_ref[...] = jnp.concatenate(parts, axis=1).astype(BF16)
    entry = thirds(entry * gain)
    long_ref[...] = jnp.broadcast_to(jnp.where(tail_is_long(docs), 1.0, 0.0), long_ref.shape)
    score = dot(write2_ref[half:], read_ref[...], NT).astype(BF16)
    send_rows = tail_is_long(doc2)
    step = min(cols // 2, 512)
    for low in range(0, cols, step):
        at = slice(low, low + step)
        to_cols = spread(heads, head_width, low, step)
        cot = (cot_ref[:, at].astype(F32) * dot(entry, to_cols)).astype(BF16)
        row = low // (cols // 2) * half
        col = low % (cols // 2)
        behind_ref[row : row + half, col : col + step] = choose(
            send_rows, cot[:half].astype(F32), dot(score, cot)
        ).astype(BF16)


def in_steps(cols, step, out_ref, held_ref, sems, columns_of):
    copies = []
    for place, low in enumerate(range(0, cols, step)):
        at = slice(low, low + step)
        held_ref[:, at] = columns_of(low, at)
        copies.append(
            pltpu.make_async_copy(held_ref.at[:, at], out_ref.at[:, at], sems.at[place])
        )
        copies[-1].start()
    for copy in copies:
        copy.wait()


def carried_kernel(
    step,
    read_ref,
    write1_ref,
    write2_ref,
    odd_ref,
    first_ref,
    then_ref,
    x2_ref,
    mixed_ref,
    entry_ref,
    exit1_ref,
    exit2_ref,
    out_ref,
    held_ref,
    sems,
):
    cols = first_ref.shape[1]
    odd = odd_ref[0, 0] == 1
    score1 = dot(read_ref[...], write1_ref[...], NT).astype(BF16)
    score2 = dot(read_ref[...], write2_ref[...], NT).astype(BF16)

    def columns_of(low, at):
        x1 = jnp.where(odd, first_ref[:, at], then_ref[:, at])
        x1 = (x1.astype(F32) * exit1_ref[:, at]).astype(BF16)
        x2 = (x2_ref[:, at].astype(F32) * exit2_ref[:, at]).astype(BF16)
        carried = dot(score2, x2) + dot(score1, x1)
        return (mixed_ref[:, at] + carried * entry_ref[:, at]).astype(BF16)

    in_steps(cols, step, out_ref, held_ref, sems, columns_of)


def returned_kernel(
    heads,
    head_width,
    step,
    write_ref,
    long_ref,
    r1_ref,
    r2_ref,
    own_ref,
    odd_ref,
    first_ref,
    then_ref,
    grad_ref,
    exit_ref,
    out_ref,
    grad_key_ref,
    grad_value_ref,
):
    tokens, cols = first_ref.shape
    state = write_ref.shape[1]
    half = tokens // 2
    odd = odd_ref[0, 0] == 1
    width = HEAD_CHANNELS
    kv2 = own_ref.shape[1]
    score1 = dot(write_ref[...], r1_ref[:, kv2 : kv2 + state], NT).astype(BF16)
    entry1 = r1_ref[:, kv2 + state : kv2 + state + 3 * heads]
    sums = dot(write_ref[...], r2_ref[:half, kv2 + cols // 2 :], NT)
    take = jnp.where(iota((tokens, half), 0) == iota((tokens, half), 1) + half, 1.0, 0.0)
    score2 = choose(long_ref[:1, :1] > 0.5, sums, take).astype(BF16)
    total = own_ref[...] + r1_ref[:, :kv2].astype(F32) + r2_ref[:, :kv2].astype(F32)
    for g in range(kv2 // (2 * width)):
        at = slice(g * width, (g + 1) * width)
        low = 2 * g * width
        grad_key_ref[:, at] = total[:, low : low + width].astype(BF16)
        grad_value_ref[:, at] = total[:, low + width : low + 2 * width].astype(BF16)

    def columns_of(low, at):
        c1 = jnp.where(odd, then_ref[:, at], first_ref[:, at])
        entry = dot(entry1, spread(heads, head_width, low, step))
        c1 = (c1.astype(F32) * entry).astype(BF16)
        row = low // (cols // 2) * half
        col = kv2 + low % (cols // 2)
        far = r2_ref[row : row + half, col : col + step]
        returned = dot(score1, c1) + dot(score2, far)
        return (grad_ref[:, at] + returned * exit_ref[:, at]).astype(BF16)

    for low in range(0, cols, step):
        at = slice(low, low + step)
        out_ref[:, at] = columns_of(low, at)

def whole(shape):
    return pl.BlockSpec(shape, lambda i: (0, 0))


def columns(rows, cols):
    return pl.BlockSpec((rows, cols), lambda i: (0, i))


def part(rows, width, low):
    return pl.BlockSpec((rows, width), lambda i: (0, low // width))


def shards(
    query_head_matrix,
    key_head_matrix,
    value_head_matrix,
    ssm_input,
    log_decay,
    state_write,
    state_read,
    document_ids,
    attention_output_gradient,
    cot_mixer,
):
    tokens, kv = key_head_matrix.shape
    kv_local = kv // HEAD_CHANNELS
    heads = log_decay.shape[1]
    state = state_write.shape[1]
    cols = ssm_input.shape[1]
    head_width = cols // heads
    group_cols = query_head_matrix.shape[1] // kv_local
    doc_row = document_ids.reshape(1, tokens)
    decay_t = log_decay.T
    aux = 4 * heads
    m_cols = 2 * kv + state + aux
    step_cols = min(512, cols)
    steps = cols // step_cols
    shape = jax.ShapeDtypeStruct
    params = pltpu.CompilerParams(vmem_limit_bytes=VMEM_LIMIT)

    odd = lax.axis_index("ctx") % 2
    m0 = pl.pallas_call(
        pack_kernel,
        out_shape=shape((tokens, m_cols), BF16),
        compiler_params=pltpu.CompilerParams(vmem_limit_bytes=PACK_LIMIT),
        name="pack",
    )(key_head_matrix, value_head_matrix, state_write, decay_t, doc_row)
    m1 = passed_along(m0, "ctx", 1)
    m2 = passed_along(m0, "ctx", 2)
    first_sent = jnp.where(odd == 0, ssm_input, cot_mixer)
    then_sent = jnp.where(odd == 0, cot_mixer, ssm_input)
    odd = odd.reshape(1, 1)
    first = exchanged(first_sent, "ctx", 0)
    then = exchanged(then_sent, "ctx", 1)
    decay_local, m1, m2 = lax.optimization_barrier((decay_t, m1, m2))
    write_at = 2 * kv
    mixed, grad, entry_w, exit_w, exit1_w, exit2_w = pl.pallas_call(
        functools.partial(local_kernel, heads, head_width),
        grid=(steps,),
        in_specs=[
            whole((1, tokens)),
            whole((tokens, state)),
            whole((tokens, state)),
            pl.BlockSpec((heads // steps, tokens), lambda i: (i, 0)),
            part(tokens, aux, write_at + state),
            part(tokens, aux, write_at + state),
            columns(tokens, step_cols),
            columns(tokens, step_cols),
        ],
        out_specs=[columns(tokens, step_cols)] * 6,
        out_shape=(shape(ssm_input.shape, F32),) * 6,
        compiler_params=params,
        name="local_mixer",
    )(doc_row, state_write, state_read, decay_local, m1, m2, ssm_input, cot_mixer)

    behind, entry_parts, long_tail = pl.pallas_call(
        functools.partial(far_kernel, head_width),
        grid=(1,),
        in_specs=[
            whole((heads, tokens)),
            whole((1, tokens)),
            whole((tokens, state)),
            part(tokens, aux, write_at + state),
            part(tokens, state, write_at),
            part(tokens, aux, write_at + state),
            whole((tokens, cols)),
        ],
        out_specs=[whole((tokens, cols // 2)), whole((tokens, aux)), whole((8, 128))],
        out_shape=(
            shape((tokens, cols // 2), BF16),
            shape((tokens, aux), BF16),
            shape((8, 128), F32),
        ),
        compiler_params=params,
        name="far",
    )(decay_t, doc_row, state_read, m1, m2, m2, cot_mixer)
    attention_out, own, back1, back2 = pl.pallas_call(
        functools.partial(attn_kernel, kv, 2 * kv + state + 3 * heads),
        grid=(kv_local,),
        in_specs=[whole((1, tokens)), whole((tokens, state))]
        + [whole((tokens, m_cols))] * 3
        + [columns(tokens, group_cols)] * 2
        + [whole((tokens, cols // 2)), whole((tokens, aux))],
        out_specs=[
            columns(tokens, group_cols),
            whole((tokens, 2 * kv)),
            whole((tokens, m_cols)),
            whole((tokens, 2 * kv + cols // 2 + state)),
        ],
        out_shape=(
            shape(query_head_matrix.shape, BF16),
            shape((tokens, 2 * kv), F32),
            shape((tokens, m_cols), BF16),
            shape((tokens, 2 * kv + cols // 2 + state), BF16),
        ),
        compiler_params=params,
        name="attention",
    )(doc_row, state_read, m0, m1, m2, query_head_matrix, attention_output_gradient, behind, entry_parts)
    r1 = passed_along(back1, "ctx", -1)
    r2 = passed_along(back2, "ctx", -2)
    x0, behind = lax.optimization_barrier((ssm_input, behind))
    x2 = passed_along(x0, "ctx", 2)


    smem = pl.BlockSpec(memory_space=pltpu.SMEM)
    half_step = min(step_cols, cols // 2)
    held = [
        pltpu.VMEM((tokens, cols), BF16),
        pltpu.SemaphoreType.DMA((cols // half_step,)),
    ]
    mixer_out = pl.pallas_call(
        functools.partial(carried_kernel, half_step),
        grid=(1,),
        in_specs=[
            whole((tokens, state)),
            part(tokens, state, write_at),
            part(tokens, state, write_at),
            smem,
        ]
        + [whole((tokens, cols))] * 7,
        out_specs=pl.BlockSpec(memory_space=pl.ANY),
        out_shape=shape(ssm_input.shape, BF16),
        scratch_shapes=held,
        compiler_params=params,
        name="carried",
    )(state_read, m1, m2, odd, first, then, x2, mixed, entry_w, exit1_w, exit2_w)

    own, mixer_out = lax.optimization_barrier((own, mixer_out))
    grad_input, grad_key, grad_value = pl.pallas_call(
        functools.partial(returned_kernel, heads, head_width, half_step),
        grid=(1,),
        in_specs=[
            whole((tokens, state)),
            whole((8, 128)),
            whole((tokens, m_cols)),
            whole((tokens, 2 * kv + cols // 2 + state)),
            whole((tokens, 2 * kv)),
            smem,
        ]
        + [whole((tokens, cols))] * 4,
        out_specs=[whole((tokens, cols))] + [whole((tokens, kv))] * 2,
        out_shape=(
            shape(cot_mixer.shape, BF16),
            shape(key_head_matrix.shape, BF16),
            shape(value_head_matrix.shape, BF16),
        ),
        compiler_params=params,
        name="returned",
    )(state_write, long_tail, r1, r2, own, odd, first, then, grad, exit_w)
    return (attention_out, mixer_out, grad_key, grad_value, grad_input)


def solution(mesh):
    return jax.shard_map(
        shards,
        mesh=mesh,
        in_specs=(
            P("ctx", "tp"),
            P("ctx", "tp"),
            P("ctx", "tp"),
            P("ctx", "tp"),
            P("ctx", "tp"),
            P("ctx", None),
            P("ctx", None),
            P("ctx"),
            P("ctx", "tp"),
            P("ctx", "tp"),
        ),
        out_specs=(P("ctx", "tp"), P("ctx", "tp"), P("ctx", "tp"), P("ctx", "tp"), P("ctx", "tp")),
        check_vma=False,
    )
```

```python
import functools
import math

import jax
import jax.numpy as jnp
from jax import lax
from jax.experimental import pallas as pl
from jax.experimental.pallas import tpu as pltpu
from jax.sharding import PartitionSpec as P

HEAD_CHANNELS = 128
BF16 = jnp.bfloat16
F32 = jnp.float32
VMEM_LIMIT = 20 * 1024 * 1024
PACK_LIMIT = 60 * 1024 * 1024
NT = (((1,), (1,)), ((), ()))
TN = (((0,), (0,)), ((), ()))


def passed_along(block, axis, distance):
    devices = range(lax.axis_size(axis))
    route = [(i - distance, i) for i in devices if i - distance in devices]
    return lax.ppermute(block, axis, route)


def exchanged(block, axis, first):
    count = lax.axis_size(axis)
    route = []
    for i in range(first, count - 1, 2):
        route += [(i, i + 1), (i + 1, i)]
    return lax.ppermute(block, axis, route)


def dot(a, b, dims=(((1,), (0,)), ((), ()))):
    return lax.dot_general(a, b, dims, preferred_element_type=F32)


def iota(shape, dim):
    return lax.broadcasted_iota(jnp.int32, shape, dim)


def split3(v):
    hi = v.astype(BF16)
    rest = v - hi.astype(F32)
    mid = rest.astype(BF16)
    lo = (rest - mid.astype(F32)).astype(BF16)
    return hi, mid, lo


def cumulative(decay_t):
    tokens = decay_t.shape[1]
    tri = iota((tokens, tokens), 0) >= iota((tokens, tokens), 1)
    tri = jnp.where(tri, 1.0, 0.0).astype(BF16)
    return sum(dot(tri, part, NT) for part in split3(decay_t))


def thirds(v):
    return jnp.concatenate([part.astype(F32) for part in split3(v)], axis=1).astype(BF16)


def spread(heads, head_width, low, cols):
    offset = iota((heads, cols), 1) + low - iota((heads, cols), 0) * head_width
    match = jnp.where((offset >= 0) & (offset < head_width), 1.0, 0.0)
    return jnp.concatenate([match] * 3, axis=0).astype(BF16)


def aux_parts(aux, heads):
    wide = aux.astype(F32)
    lam = wide[:, :heads] + wide[:, heads : 2 * heads] + wide[:, 2 * heads : 3 * heads]
    return lam, wide[:, 3 * heads : 4 * heads]


def pack_kernel(key_ref, value_ref, write_ref, decay_ref, doc_ref, m_ref):
    tokens, kv = key_ref.shape
    heads = decay_ref.shape[0]
    state = write_ref.shape[1]
    lam = cumulative(decay_ref[...])
    docs = jnp.broadcast_to(doc_ref[...].astype(F32) + 1.0, (tokens, tokens)).T[:, :heads]
    aux = jnp.concatenate([p.astype(F32) for p in split3(lam)] + [docs], axis=1).astype(BF16)
    m_ref[:, :kv] = key_ref[...]
    m_ref[:, kv : 2 * kv] = value_ref[...]
    m_ref[:, 2 * kv : 2 * kv + state] = write_ref[...]
    m_ref[:, 2 * kv + state :] = aux


def attn_kernel(
    kv,
    docs_at,
    doc_ref,
    read_ref,
    m0,
    m1,
    m2,
    q_ref,
    cot_ref,
    far_ref,
    entry_ref,
    out_ref,
    own_ref,
    back1_ref,
    back2_ref,
):
    tokens = m0.shape[0]
    group = q_ref.shape[1] // HEAD_CHANNELS
    inv_root = 1.0 / math.sqrt(HEAD_CHANNELS)
    width = HEAD_CHANNELS
    tiles = (m2, m1, m0)
    key_cols = pl.ds(pl.multiple_of(pl.program_id(0) * width, width), width)
    value_cols = pl.ds(pl.multiple_of(kv + pl.program_id(0) * width, width), width)
    keys = jnp.concatenate([tile[:, key_cols] for tile in tiles], axis=0)
    values = jnp.concatenate([tile[:, value_cols] for tile in tiles], axis=0)
    span = keys.shape[0]
    doc_s = jnp.concatenate(
        [tile[:, docs_at : docs_at + 1].astype(F32) for tile in tiles], axis=0
    )
    doc_t = doc_ref[...].astype(F32) + 1.0
    inside = (doc_s == doc_t) & (
        iota((span, tokens), 0) - (span - tokens) <= iota((span, tokens), 1)
    )
    inside = jnp.where(inside, 1.0, 0.0)
    inside = jnp.concatenate([inside] * group, axis=1) > 0.5
    query = jnp.concatenate(
        [q_ref[:, i * width : (i + 1) * width] for i in range(group)], axis=0
    )
    cot = jnp.concatenate(
        [cot_ref[:, i * width : (i + 1) * width] for i in range(group)], axis=0
    )
    score = jnp.where(inside, dot(keys, query, NT) * inv_root, -1e30)
    raised = jnp.exp(score - jnp.max(score, axis=0, keepdims=True))
    prob = (raised * (1.0 / jnp.sum(raised, axis=0, keepdims=True))).astype(BF16)
    out = dot(values, prob, TN).T
    for i in range(group):
        out_ref[:, i * width : (i + 1) * width] = out[i * tokens : (i + 1) * tokens].astype(BF16)
    prob_grad = dot(values, cot, NT)
    prob32 = prob.astype(F32)
    inner = jnp.sum(prob32 * prob_grad, axis=0, keepdims=True)
    score_grad = (prob32 * (prob_grad - inner) * inv_root).astype(BF16)
    key_grad = dot(score_grad, query)
    value_grad = dot(prob, cot)
    low = pl.multiple_of(pl.program_id(0) * 2 * width, 2 * width)
    key_at = pl.ds(low, width)
    value_at = pl.ds(pl.multiple_of(low + width, width), width)
    back2_ref[:, key_at] = key_grad[:tokens].astype(BF16)
    back2_ref[:, value_at] = value_grad[:tokens].astype(BF16)
    back1_ref[:, key_at] = key_grad[tokens : 2 * tokens].astype(BF16)
    back1_ref[:, value_at] = value_grad[tokens : 2 * tokens].astype(BF16)
    own_ref[:, key_at] = key_grad[2 * tokens :]
    own_ref[:, value_at] = value_grad[2 * tokens :]

    @pl.when(pl.program_id(0) == 0)
    def _():
        state = read_ref.shape[1]
        back1_ref[:, 2 * kv : 2 * kv + state] = read_ref[...]
        back1_ref[:, 2 * kv + state :] = entry_ref[...]
        far_cols = far_ref.shape[1]
        back2_ref[:, 2 * kv : 2 * kv + far_cols] = far_ref[...]
        back2_ref[:, 2 * kv + far_cols :] = read_ref[...]


def local_kernel(
    heads,
    head_width,
    doc_ref,
    write_ref,
    read_ref,
    decay_ref,
    aux1_ref,
    aux2_ref,
    x_ref,
    cot_ref,
    mixed_ref,
    grad_ref,
    entry_ref,
    exit_ref,
    exit1_ref,
    exit2_ref,
    spread_ref,
):
    tokens, cols = x_ref.shape
    step_heads = cols // head_width
    lam = cumulative(decay_ref[...])
    upper = iota((tokens, tokens), 0) <= iota((tokens, tokens), 1)
    upper = jnp.where(upper, 1.0, 0.0).astype(BF16)
    lam_t = sum(dot(part, upper) for part in split3(decay_ref[...]))
    doc_row = doc_ref[...].astype(F32)
    doc_col = jnp.broadcast_to(doc_row, (tokens, tokens)).T
    inside = (iota((tokens, tokens), 0) >= iota((tokens, tokens), 1)) & (doc_col == doc_row)
    score = dot(read_ref[...], write_ref[...], NT)
    lam1, doc1 = aux_parts(aux1_ref[...], heads)
    lam2, doc2 = aux_parts(aux2_ref[...], heads)
    docs = doc_col[:, :step_heads] + 1.0
    entry = jnp.exp(lam) * same(docs, last(doc1)[:, :1])
    exit_w = jnp.exp(last(lam) - lam) * same(docs, last(docs))
    to_cols = spread(step_heads, head_width, 0, cols)
    entry_ref[...] = dot(thirds(entry), to_cols)
    exit_ref[...] = dot(thirds(exit_w), to_cols)
    exit1 = jnp.exp(last(lam1) - lam1) * same(doc1, last(doc1))
    gain = jnp.exp(last(lam1)) * same(last(doc1), last(doc2))
    exit2 = jnp.exp(last(lam2) - lam2) * same(doc2, last(doc2)) * gain
    to_cols = spread(heads, head_width, pl.program_id(0) * cols, cols)
    spread_ref[...] = to_cols
    exit1_ref[...] = dot(thirds(exit1), to_cols)
    exit2_ref[...] = dot(thirds(exit2), to_cols)
    per = HEAD_CHANNELS // head_width
    lane_head = iota((tokens, HEAD_CHANNELS), 1) // head_width
    for pair in range(step_heads // per):
        at = slice(pair * HEAD_CHANNELS, (pair + 1) * HEAD_CHANNELS)
        x = x_ref[:, at]
        cot = cot_ref[:, at]
        mixed = grad = None
        for j in range(per):
            head = pair * per + j
            gap = lam[:, head : head + 1] - lam_t[head : head + 1, :]
            weights = (jnp.exp(jnp.where(inside, gap, -jnp.inf)) * score).astype(BF16)
            mixed_j = dot(weights, x)
            grad_j = dot(weights, cot, TN)
            mixed = mixed_j if j == 0 else jnp.where(lane_head == j, mixed_j, mixed)
            grad = grad_j if j == 0 else jnp.where(lane_head == j, grad_j, grad)
        mixed_ref[:, at] = mixed
        grad_ref[:, at] = grad


def same(a, b):
    return jnp.where(a == b, 1.0, 0.0)


def last(v):
    return v[v.shape[0] - 1 :]


def tail_is_long(docs):
    count = jnp.sum(same(docs[:, :1], last(docs)[:, :1]), axis=0, keepdims=True)
    return count > docs.shape[0] // 2


def choose(flag, a, b):
    return jnp.where(jnp.broadcast_to(jnp.where(flag, 1.0, 0.0), a.shape) > 0.5, a, b)


def own_numbers(decay_ref, doc_ref):
    heads, tokens = decay_ref.shape
    docs = jnp.broadcast_to(doc_ref[...].astype(F32) + 1.0, (tokens, tokens)).T
    return cumulative(decay_ref[...]), docs[:, :heads]


def far_kernel(
    head_width,
    decay_ref,
    doc_ref,
    read_ref,
    aux1_ref,
    write2_ref,
    aux2_ref,
    cot_ref,
    behind_ref,
    entry_ref,
    long_ref,
):
    tokens, cols = cot_ref.shape
    heads = decay_ref.shape[0]
    half = tokens // 2
    lam, docs = own_numbers(decay_ref, doc_ref)
    lam1, doc1 = aux_parts(aux1_ref[...], heads)
    _, doc2 = aux_parts(aux2_ref[...], heads)
    gain = jnp.exp(last(lam1)) * same(last(doc1), last(doc2))
    entry = jnp.exp(lam) * same(docs, last(doc1))
    parts = [p.astype(F32) for p in split3(entry)] + [jnp.zeros_like(entry)]
    entry_ref[...] = jnp.concatenate(parts, axis=1).astype(BF16)
    entry = thirds(entry * gain)
    long_ref[...] = jnp.broadcast_to(jnp.where(tail_is_long(docs), 1.0, 0.0), long_ref.shape)
    score = dot(write2_ref[half:], read_ref[...], NT).astype(BF16)
    send_rows = tail_is_long(doc2)
    step = min(cols // 2, 512)
    for low in range(0, cols, step):
        at = slice(low, low + step)
        to_cols = spread(heads, head_width, low, step)
        cot = (cot_ref[:, at].astype(F32) * dot(entry, to_cols)).astype(BF16)
        row = low // (cols // 2) * half
        col = low % (cols // 2)
        behind_ref[row : row + half, col : col + step] = choose(
            send_rows, cot[:half].astype(F32), dot(score, cot)
        ).astype(BF16)


def carried_kernel(
    step,
    read_ref,
    write1_ref,
    write2_ref,
    odd_ref,
    first_ref,
    then_ref,
    x2_ref,
    mixed_ref,
    entry_ref,
    exit1_ref,
    exit2_ref,
    out_ref,
):
    cols = first_ref.shape[1]
    odd = odd_ref[0, 0] == 1
    score1 = dot(read_ref[...], write1_ref[...], NT).astype(BF16)
    score2 = dot(read_ref[...], write2_ref[...], NT).astype(BF16)

    def columns_of(low, at):
        x1 = jnp.where(odd, first_ref[:, at], then_ref[:, at])
        x1 = (x1.astype(F32) * exit1_ref[:, at]).astype(BF16)
        x2 = (x2_ref[:, at].astype(F32) * exit2_ref[:, at]).astype(BF16)
        carried = dot(score2, x2) + dot(score1, x1)
        return (mixed_ref[:, at] + carried * entry_ref[:, at]).astype(BF16)

    for low in range(0, cols, step):
        at = slice(low, low + step)
        out_ref[:, at] = columns_of(low, at)


def returned_kernel(
    heads,
    head_width,
    step,
    write_ref,
    long_ref,
    r1_ref,
    r2_ref,
    own_ref,
    odd_ref,
    first_ref,
    then_ref,
    grad_ref,
    exit_ref,
    spread_ref,
    out_ref,
    grad_key_ref,
    grad_value_ref,
):
    tokens, cols = first_ref.shape
    state = write_ref.shape[1]
    half = tokens // 2
    odd = odd_ref[0, 0] == 1
    width = HEAD_CHANNELS
    kv2 = own_ref.shape[1]
    score1 = dot(write_ref[...], r1_ref[:, kv2 : kv2 + state], NT).astype(BF16)
    entry1 = r1_ref[:, kv2 + state : kv2 + state + 3 * heads]
    sums = dot(write_ref[...], r2_ref[:half, kv2 + cols // 2 :], NT)
    take = jnp.where(iota((tokens, half), 0) == iota((tokens, half), 1) + half, 1.0, 0.0)
    score2 = choose(long_ref[:1, :1] > 0.5, sums, take).astype(BF16)
    total = own_ref[...] + r1_ref[:, :kv2].astype(F32) + r2_ref[:, :kv2].astype(F32)
    for g in range(kv2 // (2 * width)):
        at = slice(g * width, (g + 1) * width)
        low = 2 * g * width
        grad_key_ref[:, at] = total[:, low : low + width].astype(BF16)
        grad_value_ref[:, at] = total[:, low + width : low + 2 * width].astype(BF16)

    def columns_of(low, at):
        c1 = jnp.where(odd, then_ref[:, at], first_ref[:, at])
        entry = dot(entry1, spread_ref[:, at])
        c1 = (c1.astype(F32) * entry).astype(BF16)
        row = low // (cols // 2) * half
        col = kv2 + low % (cols // 2)
        far = r2_ref[row : row + half, col : col + step]
        returned = dot(score1, c1) + dot(score2, far)
        return (grad_ref[:, at] + returned * exit_ref[:, at]).astype(BF16)

    for low in range(0, cols, step):
        at = slice(low, low + step)
        out_ref[:, at] = columns_of(low, at)

def whole(shape):
    return pl.BlockSpec(shape, lambda i: (0, 0))


def columns(rows, cols):
    return pl.BlockSpec((rows, cols), lambda i: (0, i))


def part(rows, width, low):
    return pl.BlockSpec((rows, width), lambda i: (0, low // width))


def shards(
    query_head_matrix,
    key_head_matrix,
    value_head_matrix,
    ssm_input,
    log_decay,
    state_write,
    state_read,
    document_ids,
    attention_output_gradient,
    cot_mixer,
):
    tokens, kv = key_head_matrix.shape
    kv_local = kv // HEAD_CHANNELS
    heads = log_decay.shape[1]
    state = state_write.shape[1]
    cols = ssm_input.shape[1]
    head_width = cols // heads
    group_cols = query_head_matrix.shape[1] // kv_local
    doc_row = document_ids.reshape(1, tokens)
    decay_t = log_decay.T
    aux = 4 * heads
    m_cols = 2 * kv + state + aux
    step_cols = min(512, cols)
    steps = cols // step_cols
    shape = jax.ShapeDtypeStruct
    params = pltpu.CompilerParams(vmem_limit_bytes=VMEM_LIMIT)

    odd = lax.axis_index("ctx") % 2
    m0 = pl.pallas_call(
        pack_kernel,
        out_shape=shape((tokens, m_cols), BF16),
        compiler_params=pltpu.CompilerParams(vmem_limit_bytes=PACK_LIMIT),
        name="pack",
    )(key_head_matrix, value_head_matrix, state_write, decay_t, doc_row)
    m1 = passed_along(m0, "ctx", 1)
    m2 = passed_along(m0, "ctx", 2)
    first_sent = jnp.where(odd == 0, ssm_input, cot_mixer)
    then_sent = jnp.where(odd == 0, cot_mixer, ssm_input)
    odd = odd.reshape(1, 1)
    first = exchanged(first_sent, "ctx", 0)
    then = exchanged(then_sent, "ctx", 1)
    decay_local, m1, m2 = lax.optimization_barrier((decay_t, m1, m2))
    write_at = 2 * kv
    mixed, grad, entry_w, exit_w, exit1_w, exit2_w, to_cols = pl.pallas_call(
        functools.partial(local_kernel, heads, head_width),
        grid=(steps,),
        in_specs=[
            whole((1, tokens)),
            whole((tokens, state)),
            whole((tokens, state)),
            pl.BlockSpec((heads // steps, tokens), lambda i: (i, 0)),
            part(tokens, aux, write_at + state),
            part(tokens, aux, write_at + state),
            columns(tokens, step_cols),
            columns(tokens, step_cols),
        ],
        out_specs=[columns(tokens, step_cols)] * 6 + [columns(3 * heads, step_cols)],
        out_shape=(shape(ssm_input.shape, F32),) * 6 + (shape((3 * heads, cols), BF16),),
        compiler_params=params,
        name="local_mixer",
    )(doc_row, state_write, state_read, decay_local, m1, m2, ssm_input, cot_mixer)

    behind, entry_parts, long_tail = pl.pallas_call(
        functools.partial(far_kernel, head_width),
        grid=(1,),
        in_specs=[
            whole((heads, tokens)),
            whole((1, tokens)),
            whole((tokens, state)),
            part(tokens, aux, write_at + state),
            part(tokens, state, write_at),
            part(tokens, aux, write_at + state),
            whole((tokens, cols)),
        ],
        out_specs=[whole((tokens, cols // 2)), whole((tokens, aux)), whole((8, 128))],
        out_shape=(
            shape((tokens, cols // 2), BF16),
            shape((tokens, aux), BF16),
            shape((8, 128), F32),
        ),
        compiler_params=params,
        name="far",
    )(decay_t, doc_row, state_read, m1, m2, m2, cot_mixer)
    attention_out, own, back1, back2 = pl.pallas_call(
        functools.partial(attn_kernel, kv, 2 * kv + state + 3 * heads),
        grid=(kv_local,),
        in_specs=[whole((1, tokens)), whole((tokens, state))]
        + [whole((tokens, m_cols))] * 3
        + [columns(tokens, group_cols)] * 2
        + [whole((tokens, cols // 2)), whole((tokens, aux))],
        out_specs=[
            columns(tokens, group_cols),
            whole((tokens, 2 * kv)),
            whole((tokens, m_cols)),
            whole((tokens, 2 * kv + cols // 2 + state)),
        ],
        out_shape=(
            shape(query_head_matrix.shape, BF16),
            shape((tokens, 2 * kv), F32),
            shape((tokens, m_cols), BF16),
            shape((tokens, 2 * kv + cols // 2 + state), BF16),
        ),
        compiler_params=params,
        name="attention",
    )(doc_row, state_read, m0, m1, m2, query_head_matrix, attention_output_gradient, behind, entry_parts)
    r1 = passed_along(back1, "ctx", -1)
    r2 = passed_along(back2, "ctx", -2)
    x0, behind = lax.optimization_barrier((ssm_input, behind))
    x2 = passed_along(x0, "ctx", 2)


    smem = pl.BlockSpec(memory_space=pltpu.SMEM)
    half_step = min(step_cols, cols // 2)
    mixer_out = pl.pallas_call(
        functools.partial(carried_kernel, half_step),
        grid=(1,),
        in_specs=[
            whole((tokens, state)),
            part(tokens, state, write_at),
            part(tokens, state, write_at),
            smem,
        ]
        + [whole((tokens, cols))] * 7,
        out_specs=whole((tokens, cols)),
        out_shape=shape(ssm_input.shape, BF16),
        compiler_params=params,
        name="carried",
    )(state_read, m1, m2, odd, first, then, x2, mixed, entry_w, exit1_w, exit2_w)

    own, mixer_out = lax.optimization_barrier((own, mixer_out))
    grad_input, grad_key, grad_value = pl.pallas_call(
        functools.partial(returned_kernel, heads, head_width, half_step),
        grid=(1,),
        in_specs=[
            whole((tokens, state)),
            whole((8, 128)),
            whole((tokens, m_cols)),
            whole((tokens, 2 * kv + cols // 2 + state)),
            whole((tokens, 2 * kv)),
            smem,
        ]
        + [whole((tokens, cols))] * 4
        + [whole((3 * heads, cols))],
        out_specs=[whole((tokens, cols))] + [whole((tokens, kv))] * 2,
        out_shape=(
            shape(cot_mixer.shape, BF16),
            shape(key_head_matrix.shape, BF16),
            shape(value_head_matrix.shape, BF16),
        ),
        compiler_params=params,
        name="returned",
    )(state_write, long_tail, r1, r2, own, odd, first, then, grad, exit_w, to_cols)
    return (attention_out, mixer_out, grad_key, grad_value, grad_input)


def solution(mesh):
    return jax.shard_map(
        shards,
        mesh=mesh,
        in_specs=(
            P("ctx", "tp"),
            P("ctx", "tp"),
            P("ctx", "tp"),
            P("ctx", "tp"),
            P("ctx", "tp"),
            P("ctx", None),
            P("ctx", None),
            P("ctx"),
            P("ctx", "tp"),
            P("ctx", "tp"),
        ),
        out_specs=(P("ctx", "tp"), P("ctx", "tp"), P("ctx", "tp"), P("ctx", "tp"), P("ctx", "tp")),
        check_vma=False,
    )
```

```python
import functools
import math

import jax
import jax.numpy as jnp
from jax import lax
from jax.experimental import pallas as pl
from jax.experimental.pallas import tpu as pltpu
from jax.sharding import PartitionSpec as P

HEAD_CHANNELS = 128
BF16 = jnp.bfloat16
F32 = jnp.float32
VMEM_LIMIT = 20 * 1024 * 1024
PACK_LIMIT = 60 * 1024 * 1024
NT = (((1,), (1,)), ((), ()))
TN = (((0,), (0,)), ((), ()))


def passed_along(block, axis, distance):
    devices = range(lax.axis_size(axis))
    route = [(i - distance, i) for i in devices if i - distance in devices]
    return lax.ppermute(block, axis, route)


def exchanged(block, axis, first):
    count = lax.axis_size(axis)
    route = []
    for i in range(first, count - 1, 2):
        route += [(i, i + 1), (i + 1, i)]
    return lax.ppermute(block, axis, route)


def dot(a, b, dims=(((1,), (0,)), ((), ()))):
    return lax.dot_general(a, b, dims, preferred_element_type=F32)


def iota(shape, dim):
    return lax.broadcasted_iota(jnp.int32, shape, dim)


def split3(v):
    hi = v.astype(BF16)
    rest = v - hi.astype(F32)
    mid = rest.astype(BF16)
    lo = (rest - mid.astype(F32)).astype(BF16)
    return hi, mid, lo


def cumulative(decay_t):
    tokens = decay_t.shape[1]
    tri = iota((tokens, tokens), 0) >= iota((tokens, tokens), 1)
    tri = jnp.where(tri, 1.0, 0.0).astype(BF16)
    return sum(dot(tri, part, NT) for part in split3(decay_t))


def thirds(v):
    return jnp.concatenate([part.astype(F32) for part in split3(v)], axis=1).astype(BF16)


def spread(heads, head_width, low, cols):
    offset = iota((heads, cols), 1) + low - iota((heads, cols), 0) * head_width
    match = jnp.where((offset >= 0) & (offset < head_width), 1.0, 0.0)
    return jnp.concatenate([match] * 3, axis=0).astype(BF16)


def aux_parts(aux, heads):
    wide = aux.astype(F32)
    lam = wide[:, :heads] + wide[:, heads : 2 * heads] + wide[:, 2 * heads : 3 * heads]
    return lam, wide[:, 3 * heads : 4 * heads]


def pack_kernel(key_ref, value_ref, write_ref, decay_ref, doc_ref, m_ref):
    tokens, kv = key_ref.shape
    heads = decay_ref.shape[0]
    state = write_ref.shape[1]
    lam = cumulative(decay_ref[...])
    docs = jnp.broadcast_to(doc_ref[...].astype(F32) + 1.0, (tokens, tokens)).T[:, :heads]
    aux = jnp.concatenate([p.astype(F32) for p in split3(lam)] + [docs], axis=1).astype(BF16)
    m_ref[:, :kv] = key_ref[...]
    m_ref[:, kv : 2 * kv] = value_ref[...]
    m_ref[:, 2 * kv : 2 * kv + state] = write_ref[...]
    m_ref[:, 2 * kv + state :] = aux


def attn_kernel(
    kv,
    docs_at,
    doc_ref,
    read_ref,
    m0,
    m1,
    m2,
    q_ref,
    cot_ref,
    far_ref,
    entry_ref,
    out_ref,
    own_ref,
    back1_ref,
    back2_ref,
):
    tokens = m0.shape[0]
    group = q_ref.shape[1] // HEAD_CHANNELS
    inv_root = 1.0 / math.sqrt(HEAD_CHANNELS)
    width = HEAD_CHANNELS
    tiles = (m2, m1, m0)
    key_cols = pl.ds(pl.multiple_of(pl.program_id(0) * width, width), width)
    value_cols = pl.ds(pl.multiple_of(kv + pl.program_id(0) * width, width), width)
    keys = jnp.concatenate([tile[:, key_cols] for tile in tiles], axis=0)
    values = jnp.concatenate([tile[:, value_cols] for tile in tiles], axis=0)
    span = keys.shape[0]
    doc_s = jnp.concatenate(
        [tile[:, docs_at : docs_at + 1].astype(F32) for tile in tiles], axis=0
    )
    doc_t = doc_ref[...].astype(F32) + 1.0
    inside = (doc_s == doc_t) & (
        iota((span, tokens), 0) - (span - tokens) <= iota((span, tokens), 1)
    )
    inside = jnp.where(inside, 1.0, 0.0)
    inside = jnp.concatenate([inside] * group, axis=1) > 0.5
    query = jnp.concatenate(
        [q_ref[:, i * width : (i + 1) * width] for i in range(group)], axis=0
    )
    cot = jnp.concatenate(
        [cot_ref[:, i * width : (i + 1) * width] for i in range(group)], axis=0
    )
    score = jnp.where(inside, dot(keys, query, NT) * inv_root, -1e30)
    raised = jnp.exp(score - jnp.max(score, axis=0, keepdims=True))
    prob = (raised * (1.0 / jnp.sum(raised, axis=0, keepdims=True))).astype(BF16)
    out = dot(values, prob, TN).T
    for i in range(group):
        out_ref[:, i * width : (i + 1) * width] = out[i * tokens : (i + 1) * tokens].astype(BF16)
    prob_grad = dot(values, cot, NT)
    prob32 = prob.astype(F32)
    inner = jnp.sum(prob32 * prob_grad, axis=0, keepdims=True)
    score_grad = (prob32 * (prob_grad - inner) * inv_root).astype(BF16)
    key_grad = dot(score_grad, query)
    value_grad = dot(prob, cot)
    low = pl.multiple_of(pl.program_id(0) * 2 * width, 2 * width)
    key_at = pl.ds(low, width)
    value_at = pl.ds(pl.multiple_of(low + width, width), width)
    back2_ref[:, key_at] = key_grad[:tokens].astype(BF16)
    back2_ref[:, value_at] = value_grad[:tokens].astype(BF16)
    back1_ref[:, key_at] = key_grad[tokens : 2 * tokens].astype(BF16)
    back1_ref[:, value_at] = value_grad[tokens : 2 * tokens].astype(BF16)
    own_ref[:, key_at] = key_grad[2 * tokens :]
    own_ref[:, value_at] = value_grad[2 * tokens :]

    @pl.when(pl.program_id(0) == 0)
    def _():
        state = read_ref.shape[1]
        back1_ref[:, 2 * kv : 2 * kv + state] = read_ref[...]
        back1_ref[:, 2 * kv + state :] = entry_ref[...]
        far_cols = far_ref.shape[1]
        back2_ref[:, 2 * kv : 2 * kv + far_cols] = far_ref[...]
        back2_ref[:, 2 * kv + far_cols :] = read_ref[...]


def local_kernel(
    heads,
    head_width,
    doc_ref,
    write_ref,
    read_ref,
    decay_ref,
    aux1_ref,
    aux2_ref,
    x_ref,
    cot_ref,
    mixed_ref,
    grad_ref,
    entry_ref,
    exit_ref,
    exit1_ref,
    exit2_ref,
):
    tokens, cols = x_ref.shape
    step_heads = cols // head_width
    lam = cumulative(decay_ref[...])
    upper = iota((tokens, tokens), 0) <= iota((tokens, tokens), 1)
    upper = jnp.where(upper, 1.0, 0.0).astype(BF16)
    lam_t = sum(dot(part, upper) for part in split3(decay_ref[...]))
    doc_row = doc_ref[...].astype(F32)
    doc_col = jnp.broadcast_to(doc_row, (tokens, tokens)).T
    inside = (iota((tokens, tokens), 0) >= iota((tokens, tokens), 1)) & (doc_col == doc_row)
    score = dot(read_ref[...], write_ref[...], NT)
    lam1, doc1 = aux_parts(aux1_ref[...], heads)
    lam2, doc2 = aux_parts(aux2_ref[...], heads)
    docs = doc_col[:, :step_heads] + 1.0
    entry = jnp.exp(lam) * same(docs, last(doc1)[:, :1])
    exit_w = jnp.exp(last(lam) - lam) * same(docs, last(docs))
    to_cols = spread(step_heads, head_width, 0, cols)
    entry_ref[...] = dot(thirds(entry), to_cols)
    exit_ref[...] = dot(thirds(exit_w), to_cols)
    exit1 = jnp.exp(last(lam1) - lam1) * same(doc1, last(doc1))
    gain = jnp.exp(last(lam1)) * same(last(doc1), last(doc2))
    exit2 = jnp.exp(last(lam2) - lam2) * same(doc2, last(doc2)) * gain
    to_cols = spread(heads, head_width, pl.program_id(0) * cols, cols)
    exit1_ref[...] = dot(thirds(exit1), to_cols)
    exit2_ref[...] = dot(thirds(exit2), to_cols)
    per = HEAD_CHANNELS // head_width
    lane_head = iota((tokens, HEAD_CHANNELS), 1) // head_width
    for pair in range(step_heads // per):
        at = slice(pair * HEAD_CHANNELS, (pair + 1) * HEAD_CHANNELS)
        x = x_ref[:, at]
        cot = cot_ref[:, at]
        mixed = grad = None
        for j in range(per):
            head = pair * per + j
            gap = lam[:, head : head + 1] - lam_t[head : head + 1, :]
            weights = (jnp.exp(jnp.where(inside, gap, -jnp.inf)) * score).astype(BF16)
            mixed_j = dot(weights, x)
            grad_j = dot(weights, cot, TN)
            mixed = mixed_j if j == 0 else jnp.where(lane_head == j, mixed_j, mixed)
            grad = grad_j if j == 0 else jnp.where(lane_head == j, grad_j, grad)
        mixed_ref[:, at] = mixed
        grad_ref[:, at] = grad


def same(a, b):
    return jnp.where(a == b, 1.0, 0.0)


def last(v):
    return v[v.shape[0] - 1 :]


def tail_is_long(docs):
    count = jnp.sum(same(docs[:, :1], last(docs)[:, :1]), axis=0, keepdims=True)
    return count > docs.shape[0] // 2


def choose(flag, a, b):
    return jnp.where(jnp.broadcast_to(jnp.where(flag, 1.0, 0.0), a.shape) > 0.5, a, b)


def own_numbers(decay_ref, doc_ref):
    heads, tokens = decay_ref.shape
    docs = jnp.broadcast_to(doc_ref[...].astype(F32) + 1.0, (tokens, tokens)).T
    return cumulative(decay_ref[...]), docs[:, :heads]


def far_kernel(
    head_width,
    decay_ref,
    doc_ref,
    read_ref,
    aux1_ref,
    write2_ref,
    aux2_ref,
    cot_ref,
    behind_ref,
    entry_ref,
    long_ref,
):
    tokens, cols = cot_ref.shape
    heads = decay_ref.shape[0]
    half = tokens // 2
    lam, docs = own_numbers(decay_ref, doc_ref)
    lam1, doc1 = aux_parts(aux1_ref[...], heads)
    _, doc2 = aux_parts(aux2_ref[...], heads)
    gain = jnp.exp(last(lam1)) * same(last(doc1), last(doc2))
    entry = jnp.exp(lam) * same(docs, last(doc1))
    parts = [p.astype(F32) for p in split3(entry)] + [jnp.zeros_like(entry)]
    entry_ref[...] = jnp.concatenate(parts, axis=1).astype(BF16)
    entry = thirds(entry * gain)
    long_ref[...] = jnp.broadcast_to(jnp.where(tail_is_long(docs), 1.0, 0.0), long_ref.shape)
    score = dot(write2_ref[half:], read_ref[...], NT).astype(BF16)
    send_rows = tail_is_long(doc2)
    step = min(cols // 2, 512)
    for low in range(0, cols, step):
        at = slice(low, low + step)
        to_cols = spread(heads, head_width, low, step)
        cot = (cot_ref[:, at].astype(F32) * dot(entry, to_cols)).astype(BF16)
        row = low // (cols // 2) * half
        col = low % (cols // 2)
        behind_ref[row : row + half, col : col + step] = choose(
            send_rows, cot[:half].astype(F32), dot(score, cot)
        ).astype(BF16)


def in_steps(cols, step, out_ref, held_ref, sems, columns_of):
    copies = []
    for place, low in enumerate(range(0, cols, step)):
        at = slice(low, low + step)
        held_ref[:, at] = columns_of(low, at)
        copies.append(
            pltpu.make_async_copy(held_ref.at[:, at], out_ref.at[:, at], sems.at[place])
        )
        copies[-1].start()
    for copy in copies:
        copy.wait()


def carried_kernel(
    step,
    read_ref,
    write1_ref,
    write2_ref,
    odd_ref,
    first_ref,
    then_ref,
    x2_ref,
    mixed_ref,
    entry_ref,
    exit1_ref,
    exit2_ref,
    out_ref,
    held_ref,
    sems,
):
    cols = first_ref.shape[1]
    odd = odd_ref[0, 0] == 1
    score1 = dot(read_ref[...], write1_ref[...], NT).astype(BF16)
    score2 = dot(read_ref[...], write2_ref[...], NT).astype(BF16)
    scores = jnp.concatenate([score1, score2], axis=1)

    def columns_of(low, at):
        x1 = jnp.where(odd, first_ref[:, at], then_ref[:, at])
        x1 = (x1.astype(F32) * exit1_ref[:, at]).astype(BF16)
        x2 = (x2_ref[:, at].astype(F32) * exit2_ref[:, at]).astype(BF16)
        carried = dot(scores, jnp.concatenate([x1, x2], axis=0))
        return (mixed_ref[:, at] + carried * entry_ref[:, at]).astype(BF16)

    in_steps(cols, step, out_ref, held_ref, sems, columns_of)


def returned_kernel(
    heads,
    head_width,
    step,
    write_ref,
    long_ref,
    r1_ref,
    r2_ref,
    own_ref,
    odd_ref,
    first_ref,
    then_ref,
    grad_ref,
    exit_ref,
    out_ref,
    grad_key_ref,
    grad_value_ref,
):
    tokens, cols = first_ref.shape
    state = write_ref.shape[1]
    half = tokens // 2
    odd = odd_ref[0, 0] == 1
    width = HEAD_CHANNELS
    kv2 = own_ref.shape[1]
    score1 = dot(write_ref[...], r1_ref[:, kv2 : kv2 + state], NT).astype(BF16)
    entry1 = r1_ref[:, kv2 + state : kv2 + state + 3 * heads]
    sums = dot(write_ref[...], r2_ref[:half, kv2 + cols // 2 :], NT)
    take = jnp.where(iota((tokens, half), 0) == iota((tokens, half), 1) + half, 1.0, 0.0)
    score2 = choose(long_ref[:1, :1] > 0.5, sums, take).astype(BF16)
    scores = jnp.concatenate([score1, score2], axis=1)
    total = own_ref[...] + r1_ref[:, :kv2].astype(F32) + r2_ref[:, :kv2].astype(F32)
    for g in range(kv2 // (2 * width)):
        at = slice(g * width, (g + 1) * width)
        low = 2 * g * width
        grad_key_ref[:, at] = total[:, low : low + width].astype(BF16)
        grad_value_ref[:, at] = total[:, low + width : low + 2 * width].astype(BF16)

    def columns_of(low, at):
        c1 = jnp.where(odd, then_ref[:, at], first_ref[:, at])
        entry = dot(entry1, spread(heads, head_width, low, step))
        c1 = (c1.astype(F32) * entry).astype(BF16)
        row = low // (cols // 2) * half
        col = kv2 + low % (cols // 2)
        far = r2_ref[row : row + half, col : col + step]
        returned = dot(scores, jnp.concatenate([c1, far], axis=0))
        return (grad_ref[:, at] + returned * exit_ref[:, at]).astype(BF16)

    for low in range(0, cols, step):
        at = slice(low, low + step)
        out_ref[:, at] = columns_of(low, at)

def whole(shape):
    return pl.BlockSpec(shape, lambda i: (0, 0))


def columns(rows, cols):
    return pl.BlockSpec((rows, cols), lambda i: (0, i))


def part(rows, width, low):
    return pl.BlockSpec((rows, width), lambda i: (0, low // width))


def shards(
    query_head_matrix,
    key_head_matrix,
    value_head_matrix,
    ssm_input,
    log_decay,
    state_write,
    state_read,
    document_ids,
    attention_output_gradient,
    cot_mixer,
):
    tokens, kv = key_head_matrix.shape
    kv_local = kv // HEAD_CHANNELS
    heads = log_decay.shape[1]
    state = state_write.shape[1]
    cols = ssm_input.shape[1]
    head_width = cols // heads
    group_cols = query_head_matrix.shape[1] // kv_local
    doc_row = document_ids.reshape(1, tokens)
    decay_t = log_decay.T
    aux = 4 * heads
    m_cols = 2 * kv + state + aux
    step_cols = min(512, cols)
    steps = cols // step_cols
    shape = jax.ShapeDtypeStruct
    params = pltpu.CompilerParams(vmem_limit_bytes=VMEM_LIMIT)

    odd = lax.axis_index("ctx") % 2
    m0 = pl.pallas_call(
        pack_kernel,
        out_shape=shape((tokens, m_cols), BF16),
        compiler_params=pltpu.CompilerParams(vmem_limit_bytes=PACK_LIMIT),
        name="pack",
    )(key_head_matrix, value_head_matrix, state_write, decay_t, doc_row)
    m1 = passed_along(m0, "ctx", 1)
    m2 = passed_along(m0, "ctx", 2)
    first_sent = jnp.where(odd == 0, ssm_input, cot_mixer)
    then_sent = jnp.where(odd == 0, cot_mixer, ssm_input)
    odd = odd.reshape(1, 1)
    first = exchanged(first_sent, "ctx", 0)
    then = exchanged(then_sent, "ctx", 1)
    decay_local, m1, m2 = lax.optimization_barrier((decay_t, m1, m2))
    write_at = 2 * kv
    mixed, grad, entry_w, exit_w, exit1_w, exit2_w = pl.pallas_call(
        functools.partial(local_kernel, heads, head_width),
        grid=(steps,),
        in_specs=[
            whole((1, tokens)),
            whole((tokens, state)),
            whole((tokens, state)),
            pl.BlockSpec((heads // steps, tokens), lambda i: (i, 0)),
            part(tokens, aux, write_at + state),
            part(tokens, aux, write_at + state),
            columns(tokens, step_cols),
            columns(tokens, step_cols),
        ],
        out_specs=[columns(tokens, step_cols)] * 6,
        out_shape=(shape(ssm_input.shape, F32),) * 6,
        compiler_params=params,
        name="local_mixer",
    )(doc_row, state_write, state_read, decay_local, m1, m2, ssm_input, cot_mixer)

    behind, entry_parts, long_tail = pl.pallas_call(
        functools.partial(far_kernel, head_width),
        grid=(1,),
        in_specs=[
            whole((heads, tokens)),
            whole((1, tokens)),
            whole((tokens, state)),
            part(tokens, aux, write_at + state),
            part(tokens, state, write_at),
            part(tokens, aux, write_at + state),
            whole((tokens, cols)),
        ],
        out_specs=[whole((tokens, cols // 2)), whole((tokens, aux)), whole((8, 128))],
        out_shape=(
            shape((tokens, cols // 2), BF16),
            shape((tokens, aux), BF16),
            shape((8, 128), F32),
        ),
        compiler_params=params,
        name="far",
    )(decay_t, doc_row, state_read, m1, m2, m2, cot_mixer)
    attention_out, own, back1, back2 = pl.pallas_call(
        functools.partial(attn_kernel, kv, 2 * kv + state + 3 * heads),
        grid=(kv_local,),
        in_specs=[whole((1, tokens)), whole((tokens, state))]
        + [whole((tokens, m_cols))] * 3
        + [columns(tokens, group_cols)] * 2
        + [whole((tokens, cols // 2)), whole((tokens, aux))],
        out_specs=[
            columns(tokens, group_cols),
            whole((tokens, 2 * kv)),
            whole((tokens, m_cols)),
            whole((tokens, 2 * kv + cols // 2 + state)),
        ],
        out_shape=(
            shape(query_head_matrix.shape, BF16),
            shape((tokens, 2 * kv), F32),
            shape((tokens, m_cols), BF16),
            shape((tokens, 2 * kv + cols // 2 + state), BF16),
        ),
        compiler_params=params,
        name="attention",
    )(doc_row, state_read, m0, m1, m2, query_head_matrix, attention_output_gradient, behind, entry_parts)
    r1 = passed_along(back1, "ctx", -1)
    r2 = passed_along(back2, "ctx", -2)
    x0, behind = lax.optimization_barrier((ssm_input, behind))
    x2 = passed_along(x0, "ctx", 2)


    smem = pl.BlockSpec(memory_space=pltpu.SMEM)
    half_step = min(step_cols, cols // 2)
    held = [
        pltpu.VMEM((tokens, cols), BF16),
        pltpu.SemaphoreType.DMA((cols // half_step,)),
    ]
    mixer_out = pl.pallas_call(
        functools.partial(carried_kernel, half_step),
        grid=(1,),
        in_specs=[
            whole((tokens, state)),
            part(tokens, state, write_at),
            part(tokens, state, write_at),
            smem,
        ]
        + [whole((tokens, cols))] * 7,
        out_specs=pl.BlockSpec(memory_space=pl.ANY),
        out_shape=shape(ssm_input.shape, BF16),
        scratch_shapes=held,
        compiler_params=params,
        name="carried",
    )(state_read, m1, m2, odd, first, then, x2, mixed, entry_w, exit1_w, exit2_w)

    own, mixer_out = lax.optimization_barrier((own, mixer_out))
    grad_input, grad_key, grad_value = pl.pallas_call(
        functools.partial(returned_kernel, heads, head_width, half_step),
        grid=(1,),
        in_specs=[
            whole((tokens, state)),
            whole((8, 128)),
            whole((tokens, m_cols)),
            whole((tokens, 2 * kv + cols // 2 + state)),
            whole((tokens, 2 * kv)),
            smem,
        ]
        + [whole((tokens, cols))] * 4,
        out_specs=[whole((tokens, cols))] + [whole((tokens, kv))] * 2,
        out_shape=(
            shape(cot_mixer.shape, BF16),
            shape(key_head_matrix.shape, BF16),
            shape(value_head_matrix.shape, BF16),
        ),
        compiler_params=params,
        name="returned",
    )(state_write, long_tail, r1, r2, own, odd, first, then, grad, exit_w)
    return (attention_out, mixer_out, grad_key, grad_value, grad_input)


def solution(mesh):
    return jax.shard_map(
        shards,
        mesh=mesh,
        in_specs=(
            P("ctx", "tp"),
            P("ctx", "tp"),
            P("ctx", "tp"),
            P("ctx", "tp"),
            P("ctx", "tp"),
            P("ctx", None),
            P("ctx", None),
            P("ctx"),
            P("ctx", "tp"),
            P("ctx", "tp"),
        ),
        out_specs=(P("ctx", "tp"), P("ctx", "tp"), P("ctx", "tp"), P("ctx", "tp"), P("ctx", "tp")),
        check_vma=False,
    )
```
